256 devices in a mesh: dp: 16 (over z, core), tensor: 16 (over x, y).
Axes of the slice: x: 4, y: 4, z: 8, core: 2. Of those that a mesh axis runs over, the one named last changes fastest.
Arguments:
- activations: bfloat16 [8192, 8192], P('dp'), may hold values from -6 to 6
- cotangent: bfloat16 [8192, 2048], P('dp', 'tensor')
- master_old: float32 [16, 16, 1032, 128], P('dp', 'tensor'), may hold values from -0.3125 to 0.3125
- first_old: float32 [16, 16, 1032, 128], P('dp', 'tensor'), may hold values from -6 to 6
- second_old: float32 [16, 16, 1032, 128], P('dp', 'tensor'), may hold values from 0.25 to 4
- old_lengths: int32 [12], replicated, may hold values from 1 to 1032, 8192 in all
- new_lengths: int32 [11], replicated, may hold values from 1 to 1120, 8192 in all
- failed: int32 [1], replicated, may hold values from 0 to 11
Outputs:
- master_new: float32 [16, 16, 1120, 128], P('dp', 'tensor')
- first_new: float32 [16, 16, 1120, 128], P('dp', 'tensor')
- second_new: float32 [16, 16, 1120, 128], P('dp', 'tensor')
- export_values: bfloat16 [16, 16, 1120, 128], P('dp', 'tensor')
- export_scales: float32 [16, 16, 4, 1120], P('dp', 'tensor')
The draws below stay inside these ranges and needn't reach their ends.
Inputs may be any that keep to these rules, and one draw needn't show every extreme that they name: `old_lengths`: whole numbers of 1 or more that sum to 8192; the largest is 1032. `new_lengths`: whole numbers of 1 or more that sum to 8192; the largest is 1120.
All inputs are finite; a program needn't handle non-finite values.
Results may differ from the reference program's by a relative error of at most 0.001.
Values sent between devices are 32-bit elements; how exact they have to be, the bound alone decides.
A program may use at most 128 MiB of HBM per device.

```python
import math
import jax
import jax.numpy as jnp
import numpy as np
from jax import lax

D = 8192
KV2 = 2048
TOK_DEV = 512
TOKENS = 8192
CW = 128
ROWS_ALL = 8192
OLD = 12
NEW = 11
CAP_OLD = 1032
CAP_NEW = 1120
N_DP = 16
N_TENSOR = 16


def draw_cotangent(key, part):
    key = jax.random.fold_in(key, 7)
    key_base, key_rows, key_cols = jax.random.split(key, 3)
    base = jax.random.normal(key_base, (TOKENS, KV2), jnp.float32)
    rows = jnp.arange(TOKENS)
    holders = max(TOKENS // TOK_DEV - 1, 1)
    rise_rows = 1.0 + 2.0 * (rows // TOK_DEV).astype(jnp.float32) / holders
    rise_cols = 1.0 + 2.0 * jnp.arange(KV2).astype(jnp.float32) / (KV2 - 1)
    row_scale = jnp.exp(jax.random.uniform(key_rows, (TOKENS,), jnp.float32) * jnp.log(10.0))
    col_scale = jnp.exp(jax.random.uniform(key_cols, (KV2,), jnp.float32) * jnp.log(10.0))
    values = 0.1 * base * (rise_rows * row_scale)[:, None] * (rise_cols * col_scale)[None, :]
    return values.astype(jnp.bfloat16)


def block_levels(key, extent, pieces, smallest, top_value):
    loudness = 1.0
    for axis_at, blocks in pieces:
        draws = jax.random.uniform(jax.random.fold_in(jax.random.fold_in(key, 6), axis_at), (blocks,), jnp.float32, smallest / len(pieces), top_value / len(pieces))
        loudness = loudness * jnp.repeat(jnp.exp(draws), extent[axis_at] // blocks).reshape((-1,) + (1,) * (len(extent) - 1 - axis_at))
    return loudness


def profile(number_of, total, limit, slope):
    weights = [(1 << 20) // math.isqrt(grade ** slope) + 1 for grade in range(2, number_of + 1)]
    surplus, counts = total - limit - (number_of - 1), [1] * (number_of - 1)
    while surplus > 0:
        free = [i for i in range(number_of - 1) if counts[i] < limit]
        pool, remaining = sum([weights[i] for i in free]), surplus
        for i in free:
            more = min(limit - counts[i], max(1, remaining * weights[i] // pool), surplus)
            counts[i] = counts[i] + more
            surplus = surplus - more
    return np.array([limit] + counts)


def ragged_sizes(key, count, total, reach, lean):
    if count == 2:
        one = jax.random.randint(key, (), max(1, total - reach), min(reach, total - 1) + 1)
        return jnp.stack([one, total - one])
    sizes = jnp.asarray(profile(count, total, reach, lean), jnp.int32)
    twos = (count - 1) // 2
    donor, sink = sizes[1:1 + 2 * twos:2], sizes[2:2 + 2 * twos:2]
    room = jnp.minimum(donor - 1, reach - sink)
    moved = jax.random.randint(jax.random.fold_in(key, 1), (twos,), 0, 1 << 20) % (room + 1)
    sizes = sizes.at[1:1 + 2 * twos:2].set(donor - moved).at[2:2 + 2 * twos:2].set(sink + moved)
    return sizes[jax.random.permutation(jax.random.fold_in(key, 2), count)]


def scatter_about(stream_key, shape, width, bound, pieces=(), held_as=jnp.bfloat16):
    array = width * jax.random.normal(stream_key, shape, jnp.float32)
    if pieces:
        array = array * block_levels(stream_key, shape, pieces, -0.22, 0.18)
    return jnp.clip(array, -bound, bound).astype(held_as)


def setup_inputs(seed: int = 0) -> dict:
    key_of = jax.random.split(jax.random.key(seed), 9)
    activations = scatter_about(key_of[0], (TOKENS, D), 1.0, 6.0, ((0, 16),))
    cotangent = draw_cotangent(jax.random.fold_in(key_of[8], 71), 0)
    master_old = scatter_about(key_of[2], (N_DP, N_TENSOR, CAP_OLD, 128), 0.02, 0.3125, ((0, 16), (1, 16)), jnp.float32)
    first_old = scatter_about(key_of[3], (N_DP, N_TENSOR, CAP_OLD, 128), 1.0, 6.0, ((0, 16), (1, 16)), jnp.float32)
    second_old = jnp.clip(jnp.exp(math.log(4.0) - 2.7725887 * jax.random.uniform(key_of[4], (N_DP, N_TENSOR, CAP_OLD, 128), jnp.float32) ** block_levels(key_of[4], (N_DP, N_TENSOR, CAP_OLD, 128), ((0, 16), (1, 16)), -0.2, 0.2)), 0.25, 4.0)
    old_lengths = ragged_sizes(key_of[5], OLD, ROWS_ALL, CAP_OLD, 2).astype(jnp.int32)
    new_lengths = ragged_sizes(key_of[6], NEW, ROWS_ALL, CAP_NEW, 2).astype(jnp.int32)
    failed = jax.random.randint(key_of[7], (1,), 0, OLD).astype(jnp.int32)
    return {"activations": activations, "cotangent": cotangent, "master_old": master_old, "first_old": first_old, "second_old": second_old, "old_lengths": old_lengths, "new_lengths": new_lengths, "failed": failed}


beta_first = 0.9
beta_second = 0.95
learn_rate = 0.004
epsilon = 1e-08
scale_floor = 0.03

def offsets(lengths):
    return (jnp.cumsum(lengths) - lengths).astype(jnp.int32)

def adam_step(master, first, second, grads):
    first = beta_first * first + (1.0 - beta_first) * grads
    second = beta_second * second + (1.0 - beta_second) * grads * grads
    correct_first = 1.0 - beta_first ** 10
    correct_second = 1.0 - beta_second ** 10
    master = master - learn_rate * (first / correct_first) / (jnp.sqrt(second / correct_second) + epsilon)
    return (master, first, second)

def export_blocks(master, live):
    blocks = master.reshape(master.shape[:-1] + (4, 32))
    largest = lax.optimization_barrier(jnp.max(jnp.abs(blocks), axis=-1))
    scale = jnp.maximum(largest, scale_floor)
    values = (blocks / scale[..., None]).reshape(master.shape)
    values = jnp.where(live[..., None], values, 0.0).astype(jnp.bfloat16)
    scales = jnp.where(live[..., None], scale, 0.0)
    return (values, jnp.swapaxes(scales, -1, -2))

def reference(activations, cotangent, master_old, first_old, second_old, old_lengths, new_lengths, failed):
    grad = jnp.dot(activations.T, cotangent, preferred_element_type=jnp.float32)
    flat = grad.reshape(D, N_TENSOR, CW).transpose(1, 0, 2).reshape(N_TENSOR, ROWS_ALL, 128)
    total = jnp.sum(flat * flat)
    clip = 1.0 / jnp.maximum(jnp.sqrt(total / float(D * KV2)), 1.0)
    lost = failed[0]
    rows = jnp.arange(ROWS_ALL, dtype=jnp.int32)
    old_start = offsets(old_lengths)
    owner = (lax.optimization_barrier(jnp.sum((rows[:, None] >= old_start[None, :]).astype(jnp.int32), axis=1)) - 1).astype(jnp.int32)
    local = (rows - old_start[owner]).astype(jnp.int32)
    holder = jnp.where(owner == lost, OLD, owner).astype(jnp.int32)

    def flatten(state):
        return jnp.transpose(state[holder, :, local, :], (1, 0, 2))
    master, first, second = adam_step(flatten(master_old), flatten(first_old), flatten(second_old), clip * flat)
    devices = jnp.arange(N_DP, dtype=jnp.int32)
    shifted = ((devices + N_DP - N_DP // 2) % N_DP).astype(jnp.int32)
    group = (shifted - (shifted > lost).astype(jnp.int32)).astype(jnp.int32)
    valid = (shifted != lost) & (group < NEW)
    group = jnp.clip(group, 0, NEW - 1).astype(jnp.int32)
    new_start = offsets(new_lengths)
    dst_start = jnp.where(valid, new_start[group], 0).astype(jnp.int32)
    dst_len = jnp.where(valid, new_lengths[group], 0).astype(jnp.int32)
    position = jnp.arange(CAP_NEW, dtype=jnp.int32)
    target = jnp.clip(dst_start[:, None] + position[None, :], 0, ROWS_ALL - 1).astype(jnp.int32)
    live = position[None, :] < dst_len[:, None]

    def place(flat_state):
        picked = jnp.transpose(flat_state[:, target], (1, 0, 2, 3))
        return jnp.where(live[:, None, :, None], picked, 0.0)
    master_new = place(master)
    first_new = place(first)
    second_new = place(second)
    values, scales = export_blocks(master_new, jnp.broadcast_to(live[:, None, :], (N_DP, N_TENSOR, CAP_NEW)))
    return (master_new, first_new, second_new, values, scales)
```

```python
import functools

import jax
import jax.numpy as jnp
from jax import lax
from jax.experimental import pallas as pl
from jax.experimental.pallas import tpu as pltpu
from jax.sharding import PartitionSpec as P

MESH = pl.DeviceIdType.MESH
beta_first = 0.9
beta_second = 0.95
learn_rate = 0.004
epsilon = 1e-08
scale_floor = 0.03

DP = 16
CHIPS = 8
OLD_GROUPS = 12
NEW_GROUPS = 11
FEATURES = 8192
TOKENS = 512
CAP_OLD = 1032
CAP_NEW = 1120
MID = 512
HALF = MID // 2
OLD_BLOCKS = 66
NEW_BLOCKS = 71
SLOT_OLD = 200
SLOT_NEW = 216
LAND = SLOT_OLD + 8
FEATURE_BLOCK = 512
F32 = jnp.float32

STREAMS = ((1, 0, 4), (-1, 1, 4), (1, 1, 3), (-1, 0, 3))
STREAM_BASE = (0, 4, 8, 11)


def prefix(ref, count):
    starts, at = [], jnp.int32(0)
    for i in range(count):
        starts.append(at)
        at = at + ref[i]
    return starts


def pick(index, values):
    result = values[0]
    for i in range(1, len(values)):
        result = jnp.where(index == i, values[i], result)
    return result


def new_group(holder, lost):
    return holder - jnp.where(holder > lost, 1, 0)


def exchange(
    act_hbm, cot_ref, master_hbm, first_hbm, second_hbm, old_ref, new_ref, lost_ref,
    out_hbm,
    act, cot_t, prod, state, send_old, land_old, sib_send, sib_land, ring_send, ring_land,
    grads, squares, squares_dp, squares_tensor, middle, send_new, starts,
    act_sem, state_sem, local_sem, old_ssem, old_rsem, sib_ssem, sib_rsem, ring_ssem, ring_rsem,
    sq_ssem, sq_rsem, new_ssem, new_rsem,
):
    dp = lax.axis_index("dp")
    tensor = lax.axis_index("tensor")
    chip = lax.div(dp, 2)
    core = lax.rem(dp, 2)
    lost = lost_ref[0]

    def remote(src, dst, ssem, rsem, to_dp, to_tensor=None):
        return pltpu.make_async_remote_copy(
            src_ref=src, dst_ref=dst, send_sem=ssem, recv_sem=rsem,
            device_id=(to_dp, tensor if to_tensor is None else to_tensor),
            device_id_type=MESH,
        )

    barrier = pltpu.get_barrier_semaphore()
    for d in range(1, DP):
        pl.semaphore_signal(
            barrier, inc=1, device_id=(lax.rem(dp + d, DP), tensor), device_id_type=MESH
        )
        pl.semaphore_signal(
            barrier, inc=1, device_id=(dp, lax.rem(tensor + d, DP)), device_id_type=MESH
        )

    state_in = [
        pltpu.make_async_copy(src, state.at[a, pl.ds(16, CAP_OLD)], state_sem.at[a])
        for a, src in enumerate((master_hbm, first_hbm, second_hbm))
    ]
    for copy in state_in:
        copy.start()
    blocks = FEATURES // FEATURE_BLOCK
    act_in = []
    for b in range(blocks):
        columns = pl.ds(b * FEATURE_BLOCK, FEATURE_BLOCK)
        act_in.append(
            pltpu.make_async_copy(act_hbm.at[:, columns], act.at[:, columns], act_sem.at[b])
        )
        act_in[-1].start()

    old_start = prefix(old_ref, OLD_GROUPS)
    new_start = prefix(new_ref, NEW_GROUPS)
    my_group = jnp.where(dp == OLD_GROUPS, lost, dp)
    my_old = pick(my_group, old_start)
    shift = 16 - lax.rem(my_old, 16)
    for h in range(OLD_GROUPS):
        g = jnp.clip(new_group(jnp.int32(h), lost), 0, NEW_GROUPS - 1)
        starts[(h + DP // 2) % DP] = pick(g, new_start)

    for copy in state_in:
        copy.wait()
    pl.semaphore_wait(barrier, 2 * (DP - 1))

    def pack_old(dst, put):
        for a in range(3):
            put(a, state[a, pl.ds(shift + dst, OLD_BLOCKS, stride=16), :])

    old_copies = []
    for d in range(1, DP):
        dst = lax.rem(dp + d, DP)
        old_copies.append(
            remote(
                send_old.at[d], land_old.at[pl.ds(dp * LAND + 8, SLOT_OLD)],
                old_ssem.at[d], old_rsem.at[d], dst,
            )
        )

    @pl.when(dp <= OLD_GROUPS)
    def _():
        for d in (8, 9, 7, 10, 6, 11, 5, 12, 4, 13, 3, 14, 2, 15, 1):
            def put(a, rows):
                send_old[d, pl.ds(a * OLD_BLOCKS, OLD_BLOCKS), :] = rows

            pack_old(lax.rem(dp + d, DP), put)
            old_copies[d - 1].start()

        def put_own(a, rows):
            land_old[pl.ds(dp * LAND + 8 + a * OLD_BLOCKS, OLD_BLOCKS), :] = rows

        pack_old(dp, put_own)

    cot_t[...] = cot_ref[...].T
    for b in range(blocks):
        act_in[b].wait()

    def multiply(b, carry):
        columns = pl.ds(pl.multiple_of(b * FEATURE_BLOCK, FEATURE_BLOCK), FEATURE_BLOCK)
        turned = jnp.dot(cot_t[...], act[:, columns], preferred_element_type=F32)
        prod[columns, :] = turned.T
        return carry

    lax.fori_loop(0, blocks, multiply, 0)

    sibling = dp + 1 - 2 * core
    sib_copies = {}
    for off in (4, 3, 5, 2, 6, 1, 7, 0):
        c = lax.rem(chip + off, CHIPS) * 2 + 1 - core
        sib_send[off] = prod[pl.ds(c, MID, stride=16), :]
        sib_copies[off] = remote(
            sib_send.at[off], sib_land.at[off], sib_ssem.at[off], sib_rsem.at[off], sibling
        )
        sib_copies[off].start()

    arrived = set()

    def partial(off, half):
        off = off % CHIPS
        if off not in arrived:
            sib_copies[off].wait_recv()
            arrived.add(off)
        c = lax.rem(chip + off, CHIPS) * 2 + core
        own = prod[pl.ds(c + 16 * HALF * half, HALF, stride=16), :]
        return own + sib_land[off, pl.ds(HALF * half, HALF), :]

    ring_copies = {}
    for k in range(1, 5):
        for s, (way, half, hops) in enumerate(STREAMS):
            if k > hops:
                continue
            n = STREAM_BASE[s] + k - 1
            total = partial(way * (hops + 1 - k), half)
            if k > 1:
                ring_copies[n - 1].wait_recv()
                total = total + ring_land[n - 1]
            ring_send[n] = total
            neighbour = lax.rem(chip + way + CHIPS, CHIPS) * 2 + core
            ring_copies[n] = remote(
                ring_send.at[n], ring_land.at[n], ring_ssem.at[n], ring_rsem.at[n], neighbour
            )
            ring_copies[n].start()
    ends = [STREAM_BASE[s] + STREAMS[s][2] - 1 for s in range(4)]
    for n in ends:
        ring_copies[n].wait_recv()
    square = jnp.zeros((8, 128), F32)
    for half in range(2):
        total = partial(0, half)
        for s in range(4):
            if STREAMS[s][1] == half:
                total = total + ring_land[ends[s]]
        grads[pl.ds(HALF * half, HALF), :] = total
        square = square + jnp.sum((total * total).reshape(HALF // 8, 8, 128), axis=0)

    def gather(mine, land, base, axis_dp):
        copies = []
        for d in range(1, DP):
            to_dp = lax.rem(dp + d, DP) if axis_dp else dp
            to_tensor = tensor if axis_dp else lax.rem(tensor + d, DP)
            copies.append(
                remote(
                    mine, land.at[d], sq_ssem.at[base + d], sq_rsem.at[base + d], to_dp, to_tensor
                )
            )
            copies[-1].start()
        return copies

    squares[0] = square
    first_gather = gather(squares.at[0], squares_dp, 0, True)
    for copy in first_gather:
        copy.wait_recv()
    for d in range(1, DP):
        square = square + squares_dp[d]
    squares[1] = square
    second_gather = gather(squares.at[1], squares_tensor, DP, False)
    for copy in second_gather:
        copy.wait_recv()
    for d in range(1, DP):
        square = square + squares_tensor[d]
    total = jnp.sum(jnp.sum(square, axis=1, keepdims=True), axis=0, keepdims=True)
    count_all = float(FEATURES * 128 * DP)
    clip = 1.0 / jnp.maximum(jnp.sqrt(total / count_all), 1.0)

    for d in range(1, DP):
        @pl.when(lax.rem(dp - d + DP, DP) <= OLD_GROUPS)
        def _():
            old_copies[d - 1].wait_recv()

    correct_first = 1.0 - beta_first**10
    correct_second = 1.0 - beta_second**10
    slots = [jnp.where(lost == i, OLD_GROUPS, i) * LAND + 8 for i in range(OLD_GROUPS)]
    old_block = [lax.div(s, 16) for s in old_start]
    old_end = [old_start[i] + old_ref[i] for i in range(OLD_GROUPS)]

    def update(m, carry):
        base = pl.multiple_of(m * 8, 8)
        row = 16 * (base + lax.broadcasted_iota(jnp.int32, (8, 128), 0)) + dp
        values = [jnp.zeros((8, 128), F32) for _ in range(3)]
        for i in range(OLD_GROUPS):
            live = (row >= old_start[i]) & (row < old_end[i])
            at = slots[i] + jnp.clip(base - old_block[i], -8, OLD_BLOCKS)
            for a in range(3):
                rows = land_old[pl.ds(at + a * OLD_BLOCKS, 8), :]
                values[a] = jnp.where(live, rows, values[a])
        master, first, second = values
        g = clip * grads[pl.ds(base, 8), :]
        first = beta_first * first + (1.0 - beta_first) * g
        second = beta_second * second + (1.0 - beta_second) * g * g
        master = master - learn_rate * (first / correct_first) / (
            jnp.sqrt(second / correct_second) + epsilon
        )
        middle[0, pl.ds(base, 8), :] = master
        middle[1, pl.ds(base, 8), :] = first
        middle[2, pl.ds(base, 8), :] = second
        return carry

    lax.fori_loop(0, MID // 8, update, 0)

    def holds(device):
        return (device >= DP // 2) | (device < DP // 2 + OLD_GROUPS - DP)

    new_copies = []
    for d in range(DP):
        dst = lax.rem(dp + d, DP)
        if d:
            copy = remote(
                send_new.at[d], out_hbm.at[dp], new_ssem.at[d], new_rsem.at[d], dst
            )
        else:
            copy = pltpu.make_async_copy(send_new.at[0], out_hbm.at[dp], local_sem)
        new_copies.append(copy)
    for d in (8, 9, 7, 10, 6, 11, 5, 12, 4, 13, 3, 14, 2, 15, 1, 0):
        dst = lax.rem(dp + d, DP)

        @pl.when(holds(dst))
        def _():
            at = lax.div(starts[dst], 16)
            for a in range(3):
                send_new[d, pl.ds(a * NEW_BLOCKS, NEW_BLOCKS), :] = middle[
                    a, pl.ds(at, NEW_BLOCKS), :
                ]
            new_copies[d].start()

    @pl.when(holds(dp))
    def _():
        for d in range(1, DP):
            new_copies[d].wait_recv()
        new_copies[0].wait()

    for d in range(1, DP):
        @pl.when(holds(lax.rem(dp + d, DP)))
        def _():
            new_copies[d].wait_send()

    @pl.when(dp <= OLD_GROUPS)
    def _():
        for copy in old_copies:
            copy.wait_send()

    for copy in list(sib_copies.values()) + list(ring_copies.values()):
        copy.wait_send()
    for copy in first_gather + second_gather:
        copy.wait_send()


def place(
    land, new_ref, lost_ref, master_ref, first_ref, second_ref, values_ref, scales_ref, rows
):
    dp = lax.axis_index("dp")
    lost = lost_ref[0]
    new_start = prefix(new_ref, NEW_GROUPS)
    holder = lax.rem(dp + DP // 2, DP)
    group = jnp.clip(new_group(holder, lost), 0, NEW_GROUPS - 1)
    held = (holder != lost) & (holder < OLD_GROUPS)
    start = pick(group, new_start)
    length = jnp.where(held, pick(group, [new_ref[i] for i in range(NEW_GROUPS)]), 0)
    for a in range(3):
        for c in range(DP):
            rows[a, pl.ds(c, NEW_BLOCKS, stride=16), :] = land[
                c, pl.ds(a * NEW_BLOCKS, NEW_BLOCKS), :
            ]
    offset = lax.rem(start, 16)
    step = 128
    for at in range(0, CAP_NEW, step):
        size = min(step, CAP_NEW - at)
        live = at + lax.broadcasted_iota(jnp.int32, (size, 128), 0) < length
        taken = [
            jnp.where(live, rows[a, pl.ds(offset + at, size), :], 0.0) for a in range(3)
        ]
        master_ref[pl.ds(at, size), :] = taken[0]
        first_ref[pl.ds(at, size), :] = taken[1]
        second_ref[pl.ds(at, size), :] = taken[2]
        turned = taken[0].T
        live_turned = at + lax.broadcasted_iota(jnp.int32, (1, size), 1) < length
        parts = []
        for b in range(4):
            block = turned[32 * b : 32 * b + 32]
            scale = jnp.maximum(jnp.max(jnp.abs(block), axis=0, keepdims=True), scale_floor)
            parts.append(block / scale)
            scales_ref[pl.ds(b, 1), pl.ds(at, size)] = jnp.where(live_turned, scale, 0.0)
        values_ref[pl.ds(at, size), :] = jnp.concatenate(parts, axis=0).T.astype(jnp.bfloat16)


def on_device(
    activations, cotangent, master_old, first_old, second_old, old_lengths, new_lengths, failed
):
    vmem = pl.BlockSpec(memory_space=pltpu.VMEM)
    smem = pl.BlockSpec(memory_space=pltpu.SMEM)
    anywhere = pl.BlockSpec(memory_space=pl.ANY)
    dma = pltpu.SemaphoreType.DMA
    landed = pl.pallas_call(
        exchange,
        out_shape=jax.ShapeDtypeStruct((DP, SLOT_NEW, 128), F32),
        in_specs=[anywhere, vmem, anywhere, anywhere, anywhere, smem, smem, smem],
        out_specs=anywhere,
        scratch_shapes=[
            pltpu.VMEM((TOKENS, FEATURES), jnp.bfloat16),
            pltpu.VMEM((128, TOKENS), jnp.bfloat16),
            pltpu.VMEM((FEATURES, 128), F32),
            pltpu.VMEM((3, CAP_OLD + 56, 128), F32),
            pltpu.VMEM((DP, SLOT_OLD, 128), F32),
            pltpu.VMEM((DP * LAND, 128), F32),
            pltpu.VMEM((CHIPS, MID, 128), F32),
            pltpu.VMEM((CHIPS, MID, 128), F32),
            pltpu.VMEM((14, HALF, 128), F32),
            pltpu.VMEM((14, HALF, 128), F32),
            pltpu.VMEM((MID, 128), F32),
            pltpu.VMEM((2, 8, 128), F32),
            pltpu.VMEM((DP, 8, 128), F32),
            pltpu.VMEM((DP, 8, 128), F32),
            pltpu.VMEM((3, MID + 80, 128), F32),
            pltpu.VMEM((DP, SLOT_NEW, 128), F32),
            pltpu.SMEM((DP,), jnp.int32),
            dma((FEATURES // FEATURE_BLOCK,)),
            dma((3,)),
            dma,
            dma((DP,)),
            dma((DP,)),
            dma((CHIPS,)),
            dma((CHIPS,)),
            dma((14,)),
            dma((14,)),
            dma((2 * DP,)),
            dma((2 * DP,)),
            dma((DP,)),
            dma((DP,)),
        ],
        compiler_params=pltpu.CompilerParams(
            collective_id=0, has_side_effects=True, vmem_limit_bytes=56 * 2**20
        ),
    )(
        activations,
        cotangent,
        master_old[0, 0],
        first_old[0, 0],
        second_old[0, 0],
        old_lengths,
        new_lengths,
        failed,
    )
    wide = jax.ShapeDtypeStruct((CAP_NEW, 128), F32)
    outs = pl.pallas_call(
        place,
        out_shape=(
            wide,
            wide,
            wide,
            jax.ShapeDtypeStruct((CAP_NEW, 128), jnp.bfloat16),
            jax.ShapeDtypeStruct((4, CAP_NEW), F32),
        ),
        in_specs=[vmem, smem, smem],
        out_specs=(vmem,) * 5,
        scratch_shapes=[pltpu.VMEM((3, NEW_BLOCKS * 16 + 16, 128), F32)],
        compiler_params=pltpu.CompilerParams(vmem_limit_bytes=32 * 2**20),
    )(landed, new_lengths, failed)
    return tuple(out[None, None] for out in outs)


def solution(mesh):
    held = P("dp", "tensor", None, None)
    return jax.shard_map(
        on_device,
        mesh=mesh,
        in_specs=(P("dp", None), P("dp", "tensor"), held, held, held, P(), P(), P()),
        out_specs=(held,) * 5,
        check_vma=False,
    )
```

```python
import functools

import jax
import jax.numpy as jnp
from jax import lax
from jax.experimental import pallas as pl
from jax.experimental.pallas import tpu as pltpu
from jax.sharding import PartitionSpec as P

MESH = pl.DeviceIdType.MESH
beta_first = 0.9
beta_second = 0.95
learn_rate = 0.004
epsilon = 1e-08
scale_floor = 0.03

DP = 16
CHIPS = 8
OLD_GROUPS = 12
NEW_GROUPS = 11
FEATURES = 8192
TOKENS = 512
CAP_OLD = 1032
CAP_NEW = 1120
MID = 512
HALF = MID // 2
OLD_BLOCKS = 66
NEW_BLOCKS = 71
SLOT_OLD = 200
SLOT_NEW = 216
LAND = SLOT_OLD + 8
FEATURE_BLOCK = 512
F32 = jnp.float32

STREAMS = ((1, 0, 4), (-1, 0, 3), (-1, 1, 4), (1, 1, 3))
STREAM_BASE = (0, 4, 7, 11)
FIRST, SECOND, MASTER = 0, 1, 2
OLD_PARTS = ((0, 72), (72, 64), (136, 64))
PART_NEW = SLOT_NEW // 3
PART_1_AFTER = 3
LATE = 7
FAR_FIRST = (8, 9, 7, 10, 6, 11, 5, 12, 4, 13, 3, 14, 2, 15, 1)
SPANS = 4


def groups_near(span):
    rows = FEATURES // SPANS
    low, high = span * rows, (span + 1) * rows
    return [
        i
        for i in range(OLD_GROUPS)
        if max(i, FEATURES - CAP_OLD * (OLD_GROUPS - i)) < high and CAP_OLD * (i + 1) > low
    ]


def prefix(ref, count):
    starts, at = [], jnp.int32(0)
    for i in range(count):
        starts.append(at)
        at = at + ref[i]
    return starts


def pick(index, values):
    result = values[0]
    for i in range(1, len(values)):
        result = jnp.where(index == i, values[i], result)
    return result


def new_group(holder, lost):
    return holder - jnp.where(holder > lost, 1, 0)


def exchange(
    act_hbm, cot_ref, master_hbm, first_hbm, second_hbm, old_ref, new_ref, lost_ref,
    out_hbm,
    act, cot_t, prod, state_0, state_1, state_2, send_old, land_old, held_old, sib_send, sib_land, ring_send, ring_land,
    grads, squares, squares_dp, squares_tensor, middle, send_new, starts,
    act_sem, state_sem, local_sem, old_ssem, old_rsem, sib_ssem, sib_rsem, ring_ssem, ring_rsem,
    sq_ssem, sq_rsem, new_ssem, new_rsem,
):
    dp = lax.axis_index("dp")
    tensor = lax.axis_index("tensor")
    chip = lax.div(dp, 2)
    core = lax.rem(dp, 2)
    lost = lost_ref[0]

    def remote(src, dst, ssem, rsem, to_dp, to_tensor=None):
        return pltpu.make_async_remote_copy(
            src_ref=src, dst_ref=dst, send_sem=ssem, recv_sem=rsem,
            device_id=(to_dp, tensor if to_tensor is None else to_tensor),
            device_id_type=MESH,
        )

    barrier = pltpu.get_barrier_semaphore()
    for d in range(1, DP):
        pl.semaphore_signal(
            barrier, inc=1, device_id=(lax.rem(dp + d, DP), tensor), device_id_type=MESH
        )
        pl.semaphore_signal(
            barrier, inc=1, device_id=(dp, lax.rem(tensor + d, DP)), device_id_type=MESH
        )

    state = (state_0, state_1, state_2)
    state_in = [
        pltpu.make_async_copy(src, state[a].at[pl.ds(16, CAP_OLD)], state_sem.at[a])
        for a, src in ((FIRST, first_hbm), (SECOND, second_hbm), (MASTER, master_hbm))
    ]
    for copy in state_in:
        copy.start()
    blocks = FEATURES // FEATURE_BLOCK
    act_in = []
    for b in range(blocks):
        columns = pl.ds(b * FEATURE_BLOCK, FEATURE_BLOCK)
        act_in.append(
            pltpu.make_async_copy(act_hbm.at[:, columns], act.at[:, columns], act_sem.at[b])
        )
        act_in[-1].start()

    old_start = prefix(old_ref, OLD_GROUPS)
    new_start = prefix(new_ref, NEW_GROUPS)
    my_group = jnp.where(dp == OLD_GROUPS, lost, dp)
    my_old = pick(my_group, old_start)
    shift = 16 - lax.rem(my_old, 16)
    for h in range(OLD_GROUPS):
        g = jnp.clip(new_group(jnp.int32(h), lost), 0, NEW_GROUPS - 1)
        starts[(h + DP // 2) % DP] = pick(g, new_start)

    sends_old = dp <= OLD_GROUPS
    old_copies = {}
    for d in range(1, DP):
        for p, (at, size) in enumerate(OLD_PARTS):
            old_copies[d, p] = remote(
                send_old.at[d, pl.ds(at, size)],
                land_old.at[pl.ds(dp * LAND + 8 + at, size)],
                old_ssem.at[p, d], old_rsem.at[p, d], lax.rem(dp + d, DP),
            )

    def pack_old(a):
        for d in FAR_FIRST:
            send_old[d, pl.ds(a * OLD_BLOCKS, OLD_BLOCKS), :] = state[a][
                pl.ds(shift + lax.rem(dp + d, DP), OLD_BLOCKS, stride=16), :
            ]
        land_old[pl.ds(dp * LAND + 8 + a * OLD_BLOCKS, OLD_BLOCKS), :] = state[a][
            pl.ds(shift + dp, OLD_BLOCKS, stride=16), :
        ]

    def start_old(p, distances=FAR_FIRST):
        @pl.when(sends_old)
        def _():
            for d in distances:
                old_copies[d, p].start()

    def land_part(p):
        for d in range(1, DP):
            @pl.when(lax.rem(dp - d + DP, DP) <= OLD_GROUPS)
            def _():
                old_copies[d, p].wait_recv()

        at, size = OLD_PARTS[p]
        for i in range(OLD_GROUPS + 1):
            rows = pl.ds(i * LAND + 8 + at, size)
            held_old[rows, :] = land_old[rows, :]

    def pack_when(a):
        state_in[a].wait()

        @pl.when(sends_old)
        def _():
            pack_old(a)

    pack_when(FIRST)
    pack_when(SECOND)
    pl.semaphore_wait(barrier, 2 * (DP - 1))
    start_old(0)

    cot_t[...] = cot_ref[...].T
    sibling = dp + 1 - 2 * core
    sib_copies = {}

    def multiply(b, carry):
        columns = pl.ds(pl.multiple_of(b * FEATURE_BLOCK, FEATURE_BLOCK), FEATURE_BLOCK)
        turned = jnp.dot(cot_t[...], act[:, columns], preferred_element_type=F32)
        prod[columns, :] = turned.T
        return carry

    def chunk(off, half, which):
        c = lax.rem(chip + off, CHIPS) * 2 + which
        return prod[pl.ds(c + 16 * HALF * half, HALF, stride=16), :]

    for half in range(2):
        for b in range(blocks // 2 * half, blocks // 2 * (half + 1)):
            act_in[b].wait()
        lax.fori_loop(blocks // 2 * half, blocks // 2 * (half + 1), multiply, 0)
        for off in (4, 3, 5, 2, 6, 1, 7, 0):
            sib_send[half, off] = chunk(off, half, 1 - core)
            copy = remote(
                sib_send.at[half, off], sib_land.at[half, off],
                sib_ssem.at[half, off], sib_rsem.at[half, off], sibling,
            )
            copy.start()
            sib_copies[off, half] = copy

    pack_when(MASTER)

    arrived = set()

    def partial(off, half):
        off = off % CHIPS
        if (off, half) not in arrived:
            sib_copies[off, half].wait_recv()
            arrived.add((off, half))
        return chunk(off, half, core) + sib_land[half, off]

    ring_copies = {}
    for k in range(1, 5):
        for s, (way, half, hops) in enumerate(STREAMS):
            if k > hops:
                continue
            n = STREAM_BASE[s] + k - 1
            total = partial(way * (hops + 1 - k), half)
            if k > 1:
                ring_copies[n - 1].wait_recv()
                total = total + ring_land[n - 1]
            ring_send[n] = total
            neighbour = lax.rem(chip + way + CHIPS, CHIPS) * 2 + core
            ring_copies[n] = remote(
                ring_send.at[n], ring_land.at[n], ring_ssem.at[n], ring_rsem.at[n], neighbour
            )
            ring_copies[n].start()
        if k == PART_1_AFTER:
            start_old(1)
    ends = [STREAM_BASE[s] + STREAMS[s][2] - 1 for s in range(4)]
    square = jnp.zeros((8, 128), F32)
    for half in range(2):
        total = partial(0, half)
        for s in range(4):
            if STREAMS[s][1] == half:
                ring_copies[ends[s]].wait_recv()
                total = total + ring_land[ends[s]]
        grads[pl.ds(HALF * half, HALF), :] = total
        square = square + jnp.sum((total * total).reshape(HALF // 8, 8, 128), axis=0)

    def gather(mine, land, base, axis_dp):
        copies = []
        for d in range(1, DP):
            to_dp = lax.rem(dp + d, DP) if axis_dp else dp
            to_tensor = tensor if axis_dp else lax.rem(tensor + d, DP)
            copies.append(
                remote(
                    mine, land.at[d], sq_ssem.at[base + d], sq_rsem.at[base + d], to_dp, to_tensor
                )
            )
            copies[-1].start()
        return copies

    slots = [jnp.where(lost == i, OLD_GROUPS, i) * LAND + 8 for i in range(OLD_GROUPS)]
    old_block = [lax.div(s, 16) for s in old_start]
    old_end = [old_start[i] + old_ref[i] for i in range(OLD_GROUPS)]
    tiles = MID // 8

    def placed(base, a, near):
        row = 16 * (base + lax.broadcasted_iota(jnp.int32, (8, 128), 0)) + dp
        value = jnp.zeros((8, 128), F32)
        for i in near:
            live = (row >= old_start[i]) & (row < old_end[i])
            at = slots[i] + jnp.clip(base - old_block[i], -8, OLD_BLOCKS)
            value = jnp.where(live, held_old[pl.ds(at + a * OLD_BLOCKS, 8), :], value)
        return value

    def each_tile(body):
        for span in range(SPANS):
            near = groups_near(span)

            def step(m, carry):
                body(pl.multiple_of(m * 8, 8), near)
                return carry

            lax.fori_loop(tiles // SPANS * span, tiles // SPANS * (span + 1), step, 0)

    def settle(a):
        def body(base, near):
            middle[a, pl.ds(base, 8), :] = placed(base, a, near)

        each_tile(body)

    squares[0] = square
    first_gather = gather(squares.at[0], squares_dp, 0, True)
    start_old(2, FAR_FIRST[:LATE])
    land_part(0)
    settle(FIRST)
    for d in range(1, DP):
        first_gather[d - 1].wait_recv()
        square = square + squares_dp[d]
    squares[1] = square
    second_gather = gather(squares.at[1], squares_tensor, DP, False)
    start_old(2, FAR_FIRST[LATE:])
    land_part(1)
    settle(SECOND)
    for d in range(1, DP):
        second_gather[d - 1].wait_recv()
        square = square + squares_tensor[d]
    total = jnp.sum(jnp.sum(square, axis=1, keepdims=True), axis=0, keepdims=True)
    count_all = float(FEATURES * 128 * DP)
    clip = 1.0 / jnp.maximum(jnp.sqrt(total / count_all), 1.0)

    def holds(device):
        return (device >= DP // 2) | (device < DP // 2 + OLD_GROUPS - DP)

    new_copies = {}
    for d in range(DP):
        for a in range(3):
            part = pl.ds(a * PART_NEW, PART_NEW)
            if d:
                new_copies[d, a] = remote(
                    send_new.at[d, part], out_hbm.at[dp, part],
                    new_ssem.at[a, d], new_rsem.at[a, d], lax.rem(dp + d, DP),
                )
            else:
                new_copies[d, a] = pltpu.make_async_copy(
                    send_new.at[0, part], out_hbm.at[dp, part], local_sem.at[a]
                )

    def start_new(arrays):
        for d in FAR_FIRST + (0,):
            dst = lax.rem(dp + d, DP)

            @pl.when(holds(dst))
            def _():
                at = lax.div(starts[dst], 16)
                for a in arrays:
                    send_new[d, pl.ds(a * PART_NEW, NEW_BLOCKS), :] = middle[
                        a, pl.ds(at, NEW_BLOCKS), :
                    ]
                    new_copies[d, a].start()

    grads[...] = clip * grads[...]
    g = grads[...]
    middle[FIRST, pl.ds(0, MID), :] = (
        beta_first * middle[FIRST, pl.ds(0, MID), :] + (1.0 - beta_first) * g
    )
    start_new((FIRST,))
    middle[SECOND, pl.ds(0, MID), :] = (
        beta_second * middle[SECOND, pl.ds(0, MID), :] + (1.0 - beta_second) * g * g
    )
    start_new((SECOND,))

    correct_first = 1.0 - beta_first**10
    correct_second = 1.0 - beta_second**10
    land_part(2)

    def step_master(base, near):
        tile = pl.ds(base, 8)
        middle[MASTER, tile, :] = placed(base, MASTER, near) - learn_rate * (
            middle[FIRST, tile, :] / correct_first
        ) / (jnp.sqrt(middle[SECOND, tile, :] / correct_second) + epsilon)

    each_tile(step_master)
    start_new((MASTER,))

    @pl.when(holds(dp))
    def _():
        for copy in [new_copies[d, a] for a in range(3) for d in range(1, DP)]:
            copy.wait_recv()
        for a in range(3):
            new_copies[0, a].wait()

    for d in range(1, DP):
        @pl.when(holds(lax.rem(dp + d, DP)))
        def _():
            for a in range(3):
                new_copies[d, a].wait_send()

    @pl.when(sends_old)
    def _():
        for copy in old_copies.values():
            copy.wait_send()

    for copy in list(sib_copies.values()) + list(ring_copies.values()):
        copy.wait_send()
    for copy in first_gather + second_gather:
        copy.wait_send()


def place(
    land, new_ref, lost_ref, master_ref, first_ref, second_ref, values_ref, scales_ref, rows
):
    dp = lax.axis_index("dp")
    lost = lost_ref[0]
    new_start = prefix(new_ref, NEW_GROUPS)
    holder = lax.rem(dp + DP // 2, DP)
    group = jnp.clip(new_group(holder, lost), 0, NEW_GROUPS - 1)
    held = (holder != lost) & (holder < OLD_GROUPS)
    start = pick(group, new_start)
    length = jnp.where(held, pick(group, [new_ref[i] for i in range(NEW_GROUPS)]), 0)
    for a in range(3):
        for c in range(DP):
            rows[a, pl.ds(c, NEW_BLOCKS, stride=16), :] = land[
                c, pl.ds(a * PART_NEW, NEW_BLOCKS), :
            ]
    offset = lax.rem(start, 16)
    step = 128
    for at in range(0, CAP_NEW, step):
        size = min(step, CAP_NEW - at)
        live = at + lax.broadcasted_iota(jnp.int32, (size, 128), 0) < length
        taken = [
            jnp.where(live, rows[a, pl.ds(offset + at, size), :], 0.0) for a in range(3)
        ]
        first_ref[pl.ds(at, size), :] = taken[FIRST]
        second_ref[pl.ds(at, size), :] = taken[SECOND]
        master_ref[pl.ds(at, size), :] = taken[MASTER]
        turned = taken[MASTER].T
        live_turned = at + lax.broadcasted_iota(jnp.int32, (1, size), 1) < length
        parts = []
        for b in range(4):
            block = turned[32 * b : 32 * b + 32]
            scale = jnp.maximum(jnp.max(jnp.abs(block), axis=0, keepdims=True), scale_floor)
            parts.append(block / scale)
            scales_ref[pl.ds(b, 1), pl.ds(at, size)] = jnp.where(live_turned, scale, 0.0)
        values_ref[pl.ds(at, size), :] = jnp.concatenate(parts, axis=0).T.astype(jnp.bfloat16)


def on_device(
    activations, cotangent, master_old, first_old, second_old, old_lengths, new_lengths, failed
):
    vmem = pl.BlockSpec(memory_space=pltpu.VMEM)
    smem = pl.BlockSpec(memory_space=pltpu.SMEM)
    anywhere = pl.BlockSpec(memory_space=pl.ANY)
    dma = pltpu.SemaphoreType.DMA
    landed = pl.pallas_call(
        exchange,
        out_shape=jax.ShapeDtypeStruct((DP, SLOT_NEW, 128), F32),
        in_specs=[anywhere, vmem, anywhere, anywhere, anywhere, smem, smem, smem],
        out_specs=anywhere,
        scratch_shapes=[
            pltpu.VMEM((TOKENS, FEATURES), jnp.bfloat16),
            pltpu.VMEM((128, TOKENS), jnp.bfloat16),
            pltpu.VMEM((FEATURES, 128), F32),
            pltpu.VMEM((CAP_OLD + 56, 128), F32),
            pltpu.VMEM((CAP_OLD + 56, 128), F32),
            pltpu.VMEM((CAP_OLD + 56, 128), F32),
            pltpu.VMEM((DP, SLOT_OLD, 128), F32),
            pltpu.VMEM((DP * LAND, 128), F32),
            pltpu.VMEM((DP * LAND, 128), F32),
            pltpu.VMEM((2, CHIPS, HALF, 128), F32),
            pltpu.VMEM((2, CHIPS, HALF, 128), F32),
            pltpu.VMEM((14, HALF, 128), F32),
            pltpu.VMEM((14, HALF, 128), F32),
            pltpu.VMEM((MID, 128), F32),
            pltpu.VMEM((2, 8, 128), F32),
            pltpu.VMEM((DP, 8, 128), F32),
            pltpu.VMEM((DP, 8, 128), F32),
            pltpu.VMEM((3, MID + 80, 128), F32),
            pltpu.VMEM((DP, SLOT_NEW, 128), F32),
            pltpu.SMEM((DP,), jnp.int32),
            dma((FEATURES // FEATURE_BLOCK,)),
            dma((3,)),
            dma((3,)),
            dma((3, DP)),
            dma((3, DP)),
            dma((2, CHIPS)),
            dma((2, CHIPS)),
            dma((14,)),
            dma((14,)),
            dma((2 * DP,)),
            dma((2 * DP,)),
            dma((3, DP)),
            dma((3, DP)),
        ],
        compiler_params=pltpu.CompilerParams(
            collective_id=0, has_side_effects=True, vmem_limit_bytes=56 * 2**20
        ),
    )(
        activations,
        cotangent,
        master_old[0, 0],
        first_old[0, 0],
        second_old[0, 0],
        old_lengths,
        new_lengths,
        failed,
    )
    wide = jax.ShapeDtypeStruct((CAP_NEW, 128), F32)
    outs = pl.pallas_call(
        place,
        out_shape=(
            wide,
            wide,
            wide,
            jax.ShapeDtypeStruct((CAP_NEW, 128), jnp.bfloat16),
            jax.ShapeDtypeStruct((4, CAP_NEW), F32),
        ),
        in_specs=[vmem, smem, smem],
        out_specs=(vmem,) * 5,
        scratch_shapes=[pltpu.VMEM((3, NEW_BLOCKS * 16 + 16, 128), F32)],
        compiler_params=pltpu.CompilerParams(vmem_limit_bytes=32 * 2**20),
    )(landed, new_lengths, failed)
    return tuple(out[None, None] for out in outs)


def solution(mesh):
    held = P("dp", "tensor", None, None)
    return jax.shard_map(
        on_device,
        mesh=mesh,
        in_specs=(P("dp", None), P("dp", "tensor"), held, held, held, P(), P(), P()),
        out_specs=(held,) * 5,
        check_vma=False,
    )
```

```python
import functools

import jax
import jax.numpy as jnp
from jax import lax
from jax.experimental import pallas as pl
from jax.experimental.pallas import tpu as pltpu
from jax.sharding import PartitionSpec as P

MESH = pl.DeviceIdType.MESH
beta_first = 0.9
beta_second = 0.95
learn_rate = 0.004
epsilon = 1e-08
scale_floor = 0.03

DP = 16
CHIPS = 8
OLD_GROUPS = 12
NEW_GROUPS = 11
FEATURES = 8192
TOKENS = 512
CAP_OLD = 1032
CAP_NEW = 1120
MID = 512
HALF = MID // 2
OLD_BLOCKS = 66
NEW_BLOCKS = 71
SLOT_OLD = 200
SLOT_NEW = 216
LAND = SLOT_OLD + 8
FEATURE_BLOCK = 512
F32 = jnp.float32

STREAMS = ((1, 0, 4), (-1, 0, 3), (-1, 1, 4), (1, 1, 3))
STREAM_BASE = (0, 4, 7, 11)
FIRST, SECOND, MASTER = 0, 1, 2
OLD_PARTS = ((0, 72), (72, 64), (136, 64))
PART_NEW = SLOT_NEW // 3
PART_1_AFTER = 3
LATE = 7
FAR_FIRST = (8, 9, 7, 10, 6, 11, 5, 12, 4, 13, 3, 14, 2, 15, 1)
SPANS = 4


def groups_near(span):
    rows = FEATURES // SPANS
    low, high = span * rows, (span + 1) * rows
    return [
        i
        for i in range(OLD_GROUPS)
        if max(i, FEATURES - CAP_OLD * (OLD_GROUPS - i)) < high and CAP_OLD * (i + 1) > low
    ]


def prefix(ref, count):
    starts, at = [], jnp.int32(0)
    for i in range(count):
        starts.append(at)
        at = at + ref[i]
    return starts


def pick(index, values):
    result = values[0]
    for i in range(1, len(values)):
        result = jnp.where(index == i, values[i], result)
    return result


def new_group(holder, lost):
    return holder - jnp.where(holder > lost, 1, 0)


def my_rows(dp, lost, new_start, new_ref):
    holder = lax.rem(dp + DP // 2, DP)
    group = jnp.clip(new_group(holder, lost), 0, NEW_GROUPS - 1)
    held = (holder != lost) & (holder < OLD_GROUPS)
    length = jnp.where(held, pick(group, [new_ref[i] for i in range(NEW_GROUPS)]), 0)
    return pick(group, new_start), length


def interleave(land, rows):
    for c in range(DP):
        rows[pl.ds(c, NEW_BLOCKS, stride=16), :] = land[c, pl.ds(0, NEW_BLOCKS), :]


def exchange(
    act_hbm, cot_hbm, master_hbm, first_hbm, second_hbm, old_ref, new_ref, lost_ref,
    first_out, second_out, land_master,
    act, cot_ref, cot_t, prod, state_0, state_1, state_2, send_old, land_old, held_old, sib_send, sib_land, ring_send, ring_land,
    grads, squares, squares_dp, squares_tensor, middle, send_new, land_first, land_second, rows, starts,
    act_sem, cot_sem, state_sem, local_sem, old_ssem, old_rsem, sib_ssem, sib_rsem, ring_ssem, ring_rsem,
    sq_ssem, sq_rsem, new_ssem, new_rsem,
):
    dp = lax.axis_index("dp")
    tensor = lax.axis_index("tensor")
    chip = lax.div(dp, 2)
    core = lax.rem(dp, 2)
    lost = lost_ref[0]

    def remote(src, dst, ssem, rsem, to_dp, to_tensor=None):
        return pltpu.make_async_remote_copy(
            src_ref=src, dst_ref=dst, send_sem=ssem, recv_sem=rsem,
            device_id=(to_dp, tensor if to_tensor is None else to_tensor),
            device_id_type=MESH,
        )

    barrier = pltpu.get_barrier_semaphore()
    for d in range(1, DP):
        pl.semaphore_signal(
            barrier, inc=1, device_id=(lax.rem(dp + d, DP), tensor), device_id_type=MESH
        )
        pl.semaphore_signal(
            barrier, inc=1, device_id=(dp, lax.rem(tensor + d, DP)), device_id_type=MESH
        )

    state = (state_0, state_1, state_2)
    state_in = [
        pltpu.make_async_copy(src, state[a].at[pl.ds(16, CAP_OLD)], state_sem.at[a])
        for a, src in ((FIRST, first_hbm), (SECOND, second_hbm), (MASTER, master_hbm))
    ]
    for copy in state_in:
        copy.start()
    cot_in = pltpu.make_async_copy(cot_hbm, cot_ref, cot_sem)
    cot_in.start()
    blocks = FEATURES // FEATURE_BLOCK
    act_in = []
    for b in range(blocks):
        columns = pl.ds(b * FEATURE_BLOCK, FEATURE_BLOCK)
        act_in.append(
            pltpu.make_async_copy(act_hbm.at[:, columns], act.at[:, columns], act_sem.at[b])
        )
        act_in[-1].start()

    old_start = prefix(old_ref, OLD_GROUPS)
    new_start = prefix(new_ref, NEW_GROUPS)
    my_group = jnp.where(dp == OLD_GROUPS, lost, dp)
    my_old = pick(my_group, old_start)
    shift = 16 - lax.rem(my_old, 16)
    for h in range(OLD_GROUPS):
        g = jnp.clip(new_group(jnp.int32(h), lost), 0, NEW_GROUPS - 1)
        starts[(h + DP // 2) % DP] = pick(g, new_start)

    sends_old = dp <= OLD_GROUPS
    old_copies = {}
    for d in range(1, DP):
        for p, (at, size) in enumerate(OLD_PARTS):
            old_copies[d, p] = remote(
                send_old.at[d, pl.ds(at, size)],
                land_old.at[pl.ds(dp * LAND + 8 + at, size)],
                old_ssem.at[p, d], old_rsem.at[p, d], lax.rem(dp + d, DP),
            )

    def pack_old(a):
        for d in FAR_FIRST:
            send_old[d, pl.ds(a * OLD_BLOCKS, OLD_BLOCKS), :] = state[a][
                pl.ds(shift + lax.rem(dp + d, DP), OLD_BLOCKS, stride=16), :
            ]
        land_old[pl.ds(dp * LAND + 8 + a * OLD_BLOCKS, OLD_BLOCKS), :] = state[a][
            pl.ds(shift + dp, OLD_BLOCKS, stride=16), :
        ]

    def start_old(p, distances=FAR_FIRST):
        @pl.when(sends_old)
        def _():
            for d in distances:
                old_copies[d, p].start()

    def land_part(p):
        for d in range(1, DP):
            @pl.when(lax.rem(dp - d + DP, DP) <= OLD_GROUPS)
            def _():
                old_copies[d, p].wait_recv()

        at, size = OLD_PARTS[p]
        for i in range(OLD_GROUPS + 1):
            rows = pl.ds(i * LAND + 8 + at, size)
            held_old[rows, :] = land_old[rows, :]

    def pack_when(a):
        state_in[a].wait()

        @pl.when(sends_old)
        def _():
            pack_old(a)

    pack_when(FIRST)
    pack_when(SECOND)
    pl.semaphore_wait(barrier, 2 * (DP - 1))
    start_old(0)

    cot_in.wait()
    cot_t[...] = cot_ref[...].T
    sibling = dp + 1 - 2 * core
    sib_copies = {}

    def multiply(b, carry):
        columns = pl.ds(pl.multiple_of(b * FEATURE_BLOCK, FEATURE_BLOCK), FEATURE_BLOCK)
        turned = jnp.dot(cot_t[...], act[:, columns], preferred_element_type=F32)
        prod[columns, :] = turned.T
        return carry

    def chunk(off, half, which):
        c = lax.rem(chip + off, CHIPS) * 2 + which
        return prod[pl.ds(c + 16 * HALF * half, HALF, stride=16), :]

    for half in range(2):
        for b in range(blocks // 2 * half, blocks // 2 * (half + 1)):
            act_in[b].wait()
        lax.fori_loop(blocks // 2 * half, blocks // 2 * (half + 1), multiply, 0)
        for off in (4, 3, 5, 2, 6, 1, 7, 0):
            sib_send[half, off] = chunk(off, half, 1 - core)
            copy = remote(
                sib_send.at[half, off], sib_land.at[half, off],
                sib_ssem.at[half, off], sib_rsem.at[half, off], sibling,
            )
            copy.start()
            sib_copies[off, half] = copy

    pack_when(MASTER)

    arrived = set()

    def partial(off, half):
        off = off % CHIPS
        if (off, half) not in arrived:
            sib_copies[off, half].wait_recv()
            arrived.add((off, half))
        return chunk(off, half, core) + sib_land[half, off]

    ring_copies = {}
    for k in range(1, 5):
        for s, (way, half, hops) in enumerate(STREAMS):
            if k > hops:
                continue
            n = STREAM_BASE[s] + k - 1
            total = partial(way * (hops + 1 - k), half)
            if k > 1:
                ring_copies[n - 1].wait_recv()
                total = total + ring_land[n - 1]
            ring_send[n] = total
            neighbour = lax.rem(chip + way + CHIPS, CHIPS) * 2 + core
            ring_copies[n] = remote(
                ring_send.at[n], ring_land.at[n], ring_ssem.at[n], ring_rsem.at[n], neighbour
            )
            ring_copies[n].start()
        if k == PART_1_AFTER:
            start_old(1)
    ends = [STREAM_BASE[s] + STREAMS[s][2] - 1 for s in range(4)]
    square = jnp.zeros((8, 128), F32)
    for half in range(2):
        total = partial(0, half)
        for s in range(4):
            if STREAMS[s][1] == half:
                ring_copies[ends[s]].wait_recv()
                total = total + ring_land[ends[s]]
        grads[pl.ds(HALF * half, HALF), :] = total
        square = square + jnp.sum((total * total).reshape(HALF // 8, 8, 128), axis=0)

    def gather(mine, land, base, axis_dp):
        copies = []
        for d in range(1, DP):
            to_dp = lax.rem(dp + d, DP) if axis_dp else dp
            to_tensor = tensor if axis_dp else lax.rem(tensor + d, DP)
            copies.append(
                remote(
                    mine, land.at[d], sq_ssem.at[base + d], sq_rsem.at[base + d], to_dp, to_tensor
                )
            )
            copies[-1].start()
        return copies

    slots = [jnp.where(lost == i, OLD_GROUPS, i) * LAND + 8 for i in range(OLD_GROUPS)]
    old_block = [lax.div(s, 16) for s in old_start]
    old_end = [old_start[i] + old_ref[i] for i in range(OLD_GROUPS)]
    tiles = MID // 8

    def placed(base, a, near):
        row = 16 * (base + lax.broadcasted_iota(jnp.int32, (8, 128), 0)) + dp
        value = jnp.zeros((8, 128), F32)
        for i in near:
            live = (row >= old_start[i]) & (row < old_end[i])
            at = slots[i] + jnp.clip(base - old_block[i], -8, OLD_BLOCKS)
            value = jnp.where(live, held_old[pl.ds(at + a * OLD_BLOCKS, 8), :], value)
        return value

    def each_tile(body):
        for span in range(SPANS):
            near = groups_near(span)

            def step(m, carry):
                body(pl.multiple_of(m * 8, 8), near)
                return carry

            lax.fori_loop(tiles // SPANS * span, tiles // SPANS * (span + 1), step, 0)

    def settle(a):
        def body(base, near):
            middle[a, pl.ds(base, 8), :] = placed(base, a, near)

        each_tile(body)

    squares[0] = square
    first_gather = gather(squares.at[0], squares_dp, 0, True)
    start_old(2, FAR_FIRST[:LATE])
    land_part(0)
    settle(FIRST)
    for d in range(1, DP):
        first_gather[d - 1].wait_recv()
        square = square + squares_dp[d]
    squares[1] = square
    second_gather = gather(squares.at[1], squares_tensor, DP, False)
    start_old(2, FAR_FIRST[LATE:])
    land_part(1)
    settle(SECOND)
    for d in range(1, DP):
        second_gather[d - 1].wait_recv()
        square = square + squares_tensor[d]
    total = jnp.sum(jnp.sum(square, axis=1, keepdims=True), axis=0, keepdims=True)
    count_all = float(FEATURES * 128 * DP)
    clip = 1.0 / jnp.maximum(jnp.sqrt(total / count_all), 1.0)

    def holds(device):
        return (device >= DP // 2) | (device < DP // 2 + OLD_GROUPS - DP)

    new_copies = {}
    for d in range(DP):
        for a, land in enumerate((land_first, land_second, land_master)):
            if d:
                new_copies[d, a] = remote(
                    send_new.at[d, a], land.at[dp],
                    new_ssem.at[a, d], new_rsem.at[a, d], lax.rem(dp + d, DP),
                )
            else:
                new_copies[d, a] = pltpu.make_async_copy(
                    send_new.at[0, a], land.at[dp], local_sem.at[a]
                )

    def start_new(arrays):
        for d in FAR_FIRST + (0,):
            dst = lax.rem(dp + d, DP)

            @pl.when(holds(dst))
            def _():
                at = lax.div(starts[dst], 16)
                for a in arrays:
                    send_new[d, a, pl.ds(0, NEW_BLOCKS), :] = middle[
                        a, pl.ds(at, NEW_BLOCKS), :
                    ]
                    new_copies[d, a].start()

    grads[...] = clip * grads[...]
    g = grads[...]
    middle[FIRST, pl.ds(0, MID), :] = (
        beta_first * middle[FIRST, pl.ds(0, MID), :] + (1.0 - beta_first) * g
    )
    start_new((FIRST,))
    middle[SECOND, pl.ds(0, MID), :] = (
        beta_second * middle[SECOND, pl.ds(0, MID), :] + (1.0 - beta_second) * g * g
    )
    start_new((SECOND,))

    correct_first = 1.0 - beta_first**10
    correct_second = 1.0 - beta_second**10
    land_part(2)

    def step_master(base, near):
        tile = pl.ds(base, 8)
        middle[MASTER, tile, :] = placed(base, MASTER, near) - learn_rate * (
            middle[FIRST, tile, :] / correct_first
        ) / (jnp.sqrt(middle[SECOND, tile, :] / correct_second) + epsilon)

    each_tile(step_master)
    start_new((MASTER,))

    start, length = my_rows(dp, lost, new_start, new_ref)

    def land_new(a):
        @pl.when(holds(dp))
        def _():
            for d in range(1, DP):
                new_copies[d, a].wait_recv()
            new_copies[0, a].wait()

    for a, land, out in ((FIRST, land_first, first_out), (SECOND, land_second, second_out)):
        land_new(a)
        interleave(land, rows.at[a])
        for at in range(0, CAP_NEW, 160):
            live = at + lax.broadcasted_iota(jnp.int32, (160, 128), 0) < length
            taken = rows[a, pl.ds(lax.rem(start, 16) + at, 160), :]
            out[pl.ds(at, 160), :] = jnp.where(live, taken, 0.0)
    land_new(MASTER)

    for d in range(1, DP):
        @pl.when(holds(lax.rem(dp + d, DP)))
        def _():
            for a in range(3):
                new_copies[d, a].wait_send()

    @pl.when(sends_old)
    def _():
        for copy in old_copies.values():
            copy.wait_send()

    for copy in list(sib_copies.values()) + list(ring_copies.values()):
        copy.wait_send()
    for copy in first_gather + second_gather:
        copy.wait_send()


def place(
    land, first, second, new_ref, lost_ref,
    master_out, first_out, second_out, values_out, scales_out,
    rows, master, values, scales, sem, master_sem, values_sem,
):
    copies = [
        pltpu.make_async_copy(first, first_out, sem.at[0]),
        pltpu.make_async_copy(second, second_out, sem.at[1]),
    ]
    for copy in copies:
        copy.start()
    start, length = my_rows(
        lax.axis_index("dp"), lost_ref[0], prefix(new_ref, NEW_GROUPS), new_ref
    )
    interleave(land, rows)
    offset = lax.rem(start, 16)
    step = 128
    for n, at in enumerate(range(0, CAP_NEW, step)):
        size = min(step, CAP_NEW - at)
        part = pl.ds(at, size)
        live = at + lax.broadcasted_iota(jnp.int32, (size, 128), 0) < length
        taken = jnp.where(live, rows[pl.ds(offset + at, size), :], 0.0)
        master[part, :] = taken
        copies.append(
            pltpu.make_async_copy(master.at[part], master_out.at[part], master_sem.at[n])
        )
        copies[-1].start()
        turned = taken.T
        live_turned = at + lax.broadcasted_iota(jnp.int32, (1, size), 1) < length
        parts = []
        for b in range(4):
            block = turned[32 * b : 32 * b + 32]
            scale = jnp.maximum(jnp.max(jnp.abs(block), axis=0, keepdims=True), scale_floor)
            parts.append(block / scale)
            scales[pl.ds(b, 1), part] = jnp.where(live_turned, scale, 0.0)
        values[part, :] = jnp.concatenate(parts, axis=0).T.astype(jnp.bfloat16)
        copies.append(
            pltpu.make_async_copy(values.at[part], values_out.at[part], values_sem.at[n])
        )
        copies[-1].start()
    copies.append(pltpu.make_async_copy(scales, scales_out, sem.at[2]))
    copies[-1].start()
    for copy in copies:
        copy.wait()


def on_device(
    activations, cotangent, master_old, first_old, second_old, old_lengths, new_lengths, failed
):
    vmem = pl.BlockSpec(memory_space=pltpu.VMEM)
    smem = pl.BlockSpec(memory_space=pltpu.SMEM)
    anywhere = pl.BlockSpec(memory_space=pl.ANY)
    dma = pltpu.SemaphoreType.DMA
    wide = jax.ShapeDtypeStruct((CAP_NEW, 128), F32)
    first, second, landed = pl.pallas_call(
        exchange,
        out_shape=(
            pltpu.VMEM((CAP_NEW, 128), F32),
            pltpu.VMEM((CAP_NEW, 128), F32),
            pltpu.VMEM((DP, PART_NEW, 128), F32),
        ),
        in_specs=[anywhere] * 5 + [smem] * 3,
        out_specs=(vmem,) * 3,
        scratch_shapes=[
            pltpu.VMEM((TOKENS, FEATURES), jnp.bfloat16),
            pltpu.VMEM((TOKENS, 128), jnp.bfloat16),
            pltpu.VMEM((128, TOKENS), jnp.bfloat16),
            pltpu.VMEM((FEATURES, 128), F32),
            pltpu.VMEM((CAP_OLD + 56, 128), F32),
            pltpu.VMEM((CAP_OLD + 56, 128), F32),
            pltpu.VMEM((CAP_OLD + 56, 128), F32),
            pltpu.VMEM((DP, SLOT_OLD, 128), F32),
            pltpu.VMEM((DP * LAND, 128), F32),
            pltpu.VMEM((DP * LAND, 128), F32),
            pltpu.VMEM((2, CHIPS, HALF, 128), F32),
            pltpu.VMEM((2, CHIPS, HALF, 128), F32),
            pltpu.VMEM((14, HALF, 128), F32),
            pltpu.VMEM((14, HALF, 128), F32),
            pltpu.VMEM((MID, 128), F32),
            pltpu.VMEM((2, 8, 128), F32),
            pltpu.VMEM((DP, 8, 128), F32),
            pltpu.VMEM((DP, 8, 128), F32),
            pltpu.VMEM((3, MID + 80, 128), F32),
            pltpu.VMEM((DP, 3, PART_NEW, 128), F32),
            pltpu.VMEM((DP, PART_NEW, 128), F32),
            pltpu.VMEM((DP, PART_NEW, 128), F32),
            pltpu.VMEM((2, NEW_BLOCKS * 16 + 16, 128), F32),
            pltpu.SMEM((DP,), jnp.int32),
            dma((FEATURES // FEATURE_BLOCK,)),
            dma,
            dma((3,)),
            dma((3,)),
            dma((3, DP)),
            dma((3, DP)),
            dma((2, CHIPS)),
            dma((2, CHIPS)),
            dma((14,)),
            dma((14,)),
            dma((2 * DP,)),
            dma((2 * DP,)),
            dma((3, DP)),
            dma((3, DP)),
        ],
        compiler_params=pltpu.CompilerParams(
            collective_id=0, has_side_effects=True, vmem_limit_bytes=56 * 2**20
        ),
    )(
        activations,
        cotangent,
        master_old[0, 0],
        first_old[0, 0],
        second_old[0, 0],
        old_lengths,
        new_lengths,
        failed,
    )
    chunks = -(-CAP_NEW // 128)
    outs = pl.pallas_call(
        place,
        out_shape=(
            wide,
            wide,
            wide,
            jax.ShapeDtypeStruct((CAP_NEW, 128), jnp.bfloat16),
            jax.ShapeDtypeStruct((4, CAP_NEW), F32),
        ),
        in_specs=[vmem, vmem, vmem, smem, smem],
        out_specs=(anywhere,) * 5,
        scratch_shapes=[
            pltpu.VMEM((NEW_BLOCKS * 16 + 16, 128), F32),
            pltpu.VMEM((CAP_NEW, 128), F32),
            pltpu.VMEM((CAP_NEW, 128), jnp.bfloat16),
            pltpu.VMEM((4, CAP_NEW), F32),
            dma((3,)),
            dma((chunks,)),
            dma((chunks,)),
        ],
        compiler_params=pltpu.CompilerParams(vmem_limit_bytes=32 * 2**20),
    )(
        *(pltpu.with_memory_space_constraint(x, pltpu.VMEM) for x in (landed, first, second)),
        new_lengths,
        failed,
    )
    return tuple(out[None, None] for out in outs)


def solution(mesh):
    held = P("dp", "tensor", None, None)
    return jax.shard_map(
        on_device,
        mesh=mesh,
        in_specs=(P("dp", None), P("dp", "tensor"), held, held, held, P(), P(), P()),
        out_specs=(held,) * 5,
        check_vma=False,
    )
```

```python
import functools

import jax
import jax.numpy as jnp
from jax import lax
from jax.experimental import pallas as pl
from jax.experimental.pallas import tpu as pltpu
from jax.sharding import PartitionSpec as P

MESH = pl.DeviceIdType.MESH
beta_first = 0.9
beta_second = 0.95
learn_rate = 0.004
epsilon = 1e-08
scale_floor = 0.03

DP = 16
CHIPS = 8
OLD_GROUPS = 12
NEW_GROUPS = 11
FEATURES = 8192
TOKENS = 512
CAP_OLD = 1032
CAP_NEW = 1120
MID = 512
HALF = MID // 2
OLD_BLOCKS = 66
NEW_BLOCKS = 71
SLOT_OLD = 200
SLOT_NEW = 216
LAND = SLOT_OLD + 8
FEATURE_BLOCK = 512
F32 = jnp.float32

STREAMS = ((1, 0, 4), (-1, 0, 3), (-1, 1, 4), (1, 1, 3))
STREAM_BASE = (0, 4, 7, 11)
FIRST, SECOND, MASTER = 0, 1, 2
OLD_PARTS = ((0, 72), (72, 64), (136, 64))
PART_NEW = SLOT_NEW // 3
PART_1_AFTER = 3
LATE = 7
FAR_FIRST = (8, 9, 7, 10, 6, 11, 5, 12, 4, 13, 3, 14, 2, 15, 1)
SPANS = 4


def groups_near(span):
    rows = FEATURES // SPANS
    low, high = span * rows, (span + 1) * rows
    return [
        i
        for i in range(OLD_GROUPS)
        if max(i, FEATURES - CAP_OLD * (OLD_GROUPS - i)) < high and CAP_OLD * (i + 1) > low
    ]


def prefix(ref, count):
    starts, at = [], jnp.int32(0)
    for i in range(count):
        starts.append(at)
        at = at + ref[i]
    return starts


def pick(index, values):
    result = values[0]
    for i in range(1, len(values)):
        result = jnp.where(index == i, values[i], result)
    return result


def new_group(holder, lost):
    return holder - jnp.where(holder > lost, 1, 0)


def my_rows(dp, lost, new_start, new_ref):
    holder = lax.rem(dp + DP // 2, DP)
    group = jnp.clip(new_group(holder, lost), 0, NEW_GROUPS - 1)
    held = (holder != lost) & (holder < OLD_GROUPS)
    length = jnp.where(held, pick(group, [new_ref[i] for i in range(NEW_GROUPS)]), 0)
    return pick(group, new_start), length


def exchange(
    act_hbm, cot_hbm, master_hbm, first_hbm, second_hbm, old_hbm, new_hbm, lost_hbm,
    first_out, second_out, rows_master, held_out,
    act, cot_ref, cot_t, prod, state_0, state_1, state_2, send_old, land_old, held_old, sib_send, sib_land, ring_send, ring_land,
    grads, squares, squares_dp, squares_tensor, middle, send_new, land_first, land_second, land_master, rows, starts,
    old_ref, new_ref, lost_ref, table_sem,
    act_sem, cot_sem, state_sem, local_sem, old_ssem, old_rsem, sib_ssem, sib_rsem, ring_ssem, ring_rsem,
    sq_ssem, sq_rsem, new_ssem, new_rsem,
):
    dp = lax.axis_index("dp")
    tensor = lax.axis_index("tensor")
    chip = lax.div(dp, 2)
    core = lax.rem(dp, 2)

    def remote(src, dst, ssem, rsem, to_dp, to_tensor=None):
        return pltpu.make_async_remote_copy(
            src_ref=src, dst_ref=dst, send_sem=ssem, recv_sem=rsem,
            device_id=(to_dp, tensor if to_tensor is None else to_tensor),
            device_id_type=MESH,
        )

    barrier = pltpu.get_barrier_semaphore()
    for d in FAR_FIRST:
        pl.semaphore_signal(
            barrier, inc=1, device_id=(lax.rem(dp + d, DP), tensor), device_id_type=MESH
        )
    for d in FAR_FIRST:
        pl.semaphore_signal(
            barrier, inc=1, device_id=(dp, lax.rem(tensor + d, DP)), device_id_type=MESH
        )

    tables = [
        pltpu.make_async_copy(src, dst, table_sem.at[n])
        for n, (src, dst) in enumerate(
            ((old_hbm, old_ref), (new_hbm, new_ref), (lost_hbm, lost_ref))
        )
    ]
    for copy in tables:
        copy.start()
    state = (state_0, state_1, state_2)
    state_in = [
        pltpu.make_async_copy(src, state[a].at[pl.ds(16, CAP_OLD)], state_sem.at[a])
        for a, src in ((FIRST, first_hbm), (SECOND, second_hbm), (MASTER, master_hbm))
    ]
    for copy in state_in:
        copy.start()
    cot_in = pltpu.make_async_copy(cot_hbm, cot_ref, cot_sem)
    cot_in.start()
    blocks = FEATURES // FEATURE_BLOCK
    act_in = []
    for b in range(blocks):
        columns = pl.ds(b * FEATURE_BLOCK, FEATURE_BLOCK)
        act_in.append(
            pltpu.make_async_copy(act_hbm.at[:, columns], act.at[:, columns], act_sem.at[b])
        )
        act_in[-1].start()

    for copy in tables:
        copy.wait()
    lost = lost_ref[0]
    old_start = prefix(old_ref, OLD_GROUPS)
    new_start = prefix(new_ref, NEW_GROUPS)
    my_group = jnp.where(dp == OLD_GROUPS, lost, dp)
    my_old = pick(my_group, old_start)
    shift = 16 - lax.rem(my_old, 16)
    for h in range(OLD_GROUPS):
        g = jnp.clip(new_group(jnp.int32(h), lost), 0, NEW_GROUPS - 1)
        starts[(h + DP // 2) % DP] = pick(g, new_start)

    sends_old = dp <= OLD_GROUPS
    old_copies = {}
    for d in range(1, DP):
        for p, (at, size) in enumerate(OLD_PARTS):
            old_copies[d, p] = remote(
                send_old.at[d, pl.ds(at, size)],
                land_old.at[pl.ds(dp * LAND + 8 + at, size)],
                old_ssem.at[p, d], old_rsem.at[p, d], lax.rem(dp + d, DP),
            )

    def pack_old(a):
        for d in FAR_FIRST:
            send_old[d, pl.ds(a * OLD_BLOCKS, OLD_BLOCKS), :] = state[a][
                pl.ds(shift + lax.rem(dp + d, DP), OLD_BLOCKS, stride=16), :
            ]
        land_old[pl.ds(dp * LAND + 8 + a * OLD_BLOCKS, OLD_BLOCKS), :] = state[a][
            pl.ds(shift + dp, OLD_BLOCKS, stride=16), :
        ]

    def start_old(p, distances=FAR_FIRST):
        @pl.when(sends_old)
        def _():
            for d in distances:
                old_copies[d, p].start()

    def land_part(p):
        for d in range(1, DP):
            @pl.when(lax.rem(dp - d + DP, DP) <= OLD_GROUPS)
            def _():
                old_copies[d, p].wait_recv()

        at, size = OLD_PARTS[p]
        for i in range(OLD_GROUPS + 1):
            rows = pl.ds(i * LAND + 8 + at, size)
            held_old[rows, :] = land_old[rows, :]

    def pack_when(a):
        state_in[a].wait()

        @pl.when(sends_old)
        def _():
            pack_old(a)

    pack_when(FIRST)
    pack_when(SECOND)
    pl.semaphore_wait(barrier, 2 * (DP - 1))
    start_old(0)
    pack_when(MASTER)

    cot_in.wait()
    cot_t[...] = cot_ref[...].T
    sibling = dp + 1 - 2 * core
    sib_copies = {}

    def multiply(b, carry):
        columns = pl.ds(pl.multiple_of(b * FEATURE_BLOCK, FEATURE_BLOCK), FEATURE_BLOCK)
        turned = jnp.dot(cot_t[...], act[:, columns], preferred_element_type=F32)
        prod[columns, :] = turned.T
        return carry

    def chunk(off, half, which):
        c = lax.rem(chip + off, CHIPS) * 2 + which
        return prod[pl.ds(c + 16 * HALF * half, HALF, stride=16), :]

    for half in range(2):
        for b in range(blocks // 2 * half, blocks // 2 * (half + 1)):
            act_in[b].wait()
        lax.fori_loop(blocks // 2 * half, blocks // 2 * (half + 1), multiply, 0)
        for off in (4, 3, 5, 2, 6, 1, 7, 0):
            sib_send[half, off] = chunk(off, half, 1 - core)
            copy = remote(
                sib_send.at[half, off], sib_land.at[half, off],
                sib_ssem.at[half, off], sib_rsem.at[half, off], sibling,
            )
            copy.start()
            sib_copies[off, half] = copy


    arrived = set()

    def partial(off, half):
        off = off % CHIPS
        if (off, half) not in arrived:
            sib_copies[off, half].wait_recv()
            arrived.add((off, half))
        return chunk(off, half, core) + sib_land[half, off]

    ring_copies = {}
    for k in range(1, 5):
        for s, (way, half, hops) in enumerate(STREAMS):
            if k > hops:
                continue
            n = STREAM_BASE[s] + k - 1
            total = partial(way * (hops + 1 - k), half)
            if k > 1:
                ring_copies[n - 1].wait_recv()
                total = total + ring_land[n - 1]
            ring_send[n] = total
            neighbour = lax.rem(chip + way + CHIPS, CHIPS) * 2 + core
            ring_copies[n] = remote(
                ring_send.at[n], ring_land.at[n], ring_ssem.at[n], ring_rsem.at[n], neighbour
            )
            ring_copies[n].start()
        if k == PART_1_AFTER:
            start_old(1)
    ends = [STREAM_BASE[s] + STREAMS[s][2] - 1 for s in range(4)]
    square = jnp.zeros((8, 128), F32)
    for half in range(2):
        total = partial(0, half)
        for s in range(4):
            if STREAMS[s][1] == half:
                ring_copies[ends[s]].wait_recv()
                total = total + ring_land[ends[s]]
        grads[pl.ds(HALF * half, HALF), :] = total
        square = square + jnp.sum((total * total).reshape(HALF // 8, 8, 128), axis=0)

    def gather(mine, land, base, axis_dp):
        copies = []
        for d in range(1, DP):
            to_dp = lax.rem(dp + d, DP) if axis_dp else dp
            to_tensor = tensor if axis_dp else lax.rem(tensor + d, DP)
            copies.append(
                remote(
                    mine, land.at[d], sq_ssem.at[base + d], sq_rsem.at[base + d], to_dp, to_tensor
                )
            )
            copies[-1].start()
        return copies

    slots = [jnp.where(lost == i, OLD_GROUPS, i) * LAND + 8 for i in range(OLD_GROUPS)]
    old_block = [lax.div(s, 16) for s in old_start]
    old_end = [old_start[i] + old_ref[i] for i in range(OLD_GROUPS)]
    tiles = MID // 8

    def placed(base, a, near):
        row = 16 * (base + lax.broadcasted_iota(jnp.int32, (8, 128), 0)) + dp
        value = jnp.zeros((8, 128), F32)
        for i in near:
            live = (row >= old_start[i]) & (row < old_end[i])
            at = slots[i] + jnp.clip(base - old_block[i], -8, OLD_BLOCKS)
            value = jnp.where(live, held_old[pl.ds(at + a * OLD_BLOCKS, 8), :], value)
        return value

    def each_tile(body):
        for span in range(SPANS):
            near = groups_near(span)

            def step(m, carry):
                body(pl.multiple_of(m * 8, 8), near)
                return carry

            lax.fori_loop(tiles // SPANS * span, tiles // SPANS * (span + 1), step, 0)

    def settle(a):
        def body(base, near):
            middle[a, pl.ds(base, 8), :] = placed(base, a, near)

        each_tile(body)

    squares[0] = square
    first_gather = gather(squares.at[0], squares_dp, 0, True)
    start_old(2, FAR_FIRST[:LATE])
    land_part(0)
    settle(FIRST)
    for d in range(1, DP):
        first_gather[d - 1].wait_recv()
        square = square + squares_dp[d]
    squares[1] = square
    second_gather = gather(squares.at[1], squares_tensor, DP, False)
    start_old(2, FAR_FIRST[LATE:])
    land_part(1)
    settle(SECOND)
    for d in range(1, DP):
        second_gather[d - 1].wait_recv()
        square = square + squares_tensor[d]
    total = jnp.sum(jnp.sum(square, axis=1, keepdims=True), axis=0, keepdims=True)
    count_all = float(FEATURES * 128 * DP)
    clip = 1.0 / jnp.maximum(jnp.sqrt(total / count_all), 1.0)

    def holds(device):
        return (device >= DP // 2) | (device < DP // 2 + OLD_GROUPS - DP)

    new_copies = {}
    for d in range(DP):
        for a, land in enumerate((land_first, land_second, land_master)):
            if d:
                new_copies[d, a] = remote(
                    send_new.at[d, a], land.at[dp],
                    new_ssem.at[a, d], new_rsem.at[a, d], lax.rem(dp + d, DP),
                )
            else:
                new_copies[d, a] = pltpu.make_async_copy(
                    send_new.at[0, a], land.at[dp], local_sem.at[a]
                )

    def start_new(arrays):
        for d in FAR_FIRST + (0,):
            dst = lax.rem(dp + d, DP)

            @pl.when(holds(dst))
            def _():
                at = lax.div(starts[dst], 16)
                for a in arrays:
                    send_new[d, a, pl.ds(0, NEW_BLOCKS), :] = middle[
                        a, pl.ds(at, NEW_BLOCKS), :
                    ]
                    new_copies[d, a].start()

    g = clip * grads[...]
    middle[FIRST, pl.ds(0, MID), :] = (
        beta_first * middle[FIRST, pl.ds(0, MID), :] + (1.0 - beta_first) * g
    )
    start_new((FIRST,))
    middle[SECOND, pl.ds(0, MID), :] = (
        beta_second * middle[SECOND, pl.ds(0, MID), :] + (1.0 - beta_second) * g * g
    )
    start_new((SECOND,))

    correct_first = 1.0 - beta_first**10
    correct_second = 1.0 - beta_second**10
    land_part(2)

    def step_master(base, near):
        tile = pl.ds(base, 8)
        middle[MASTER, tile, :] = placed(base, MASTER, near) - learn_rate * (
            middle[FIRST, tile, :] / correct_first
        ) / (jnp.sqrt(middle[SECOND, tile, :] / correct_second) + epsilon)

    each_tile(step_master)
    start_new((MASTER,))

    @pl.when(sends_old)
    def _():
        for copy in old_copies.values():
            copy.wait_send()

    for copy in list(sib_copies.values()) + list(ring_copies.values()):
        copy.wait_send()
    for copy in first_gather + second_gather:
        copy.wait_send()

    start, length = my_rows(dp, lost, new_start, new_ref)
    held_out[0] = lax.rem(start, 16)
    held_out[1] = length

    def land_new(a, land, out):
        @pl.when(holds(dp))
        def _():
            for d in (0, 1, 15, 2, 14, 3, 13, 4, 12, 5, 11, 6, 10, 7, 9, 8):
                if d:
                    new_copies[d, a].wait_recv()
                else:
                    new_copies[0, a].wait()
                c = lax.rem(dp - d + DP, DP)
                out[pl.ds(c, NEW_BLOCKS, stride=16), :] = land[c, pl.ds(0, NEW_BLOCKS), :]

    for a, land, out in ((FIRST, land_first, first_out), (SECOND, land_second, second_out)):
        land_new(a, land, rows.at[a])
        for at in range(0, CAP_NEW, 160):
            live = at + lax.broadcasted_iota(jnp.int32, (160, 128), 0) < length
            taken = rows[a, pl.ds(lax.rem(start, 16) + at, 160), :]
            out[pl.ds(at, 160), :] = jnp.where(live, taken, 0.0)
    for d in range(1, DP):
        @pl.when(holds(lax.rem(dp + d, DP)))
        def _():
            for a in range(3):
                new_copies[d, a].wait_send()

    land_new(MASTER, land_master, rows_master)


def place(
    rows, first, second, held_ref,
    master_out, first_out, second_out, values_out, scales_out,
    master, values, scales, sem, master_sem, values_sem,
):
    copies = [
        pltpu.make_async_copy(first, first_out, sem.at[0]),
        pltpu.make_async_copy(second, second_out, sem.at[1]),
    ]
    for copy in copies:
        copy.start()
    offset = held_ref[0]
    length = held_ref[1]
    step = 128
    for n, at in enumerate(range(0, CAP_NEW, step)):
        size = min(step, CAP_NEW - at)
        part = pl.ds(at, size)
        live = at + lax.broadcasted_iota(jnp.int32, (size, 128), 0) < length
        taken = jnp.where(live, rows[pl.ds(offset + at, size), :], 0.0)
        master[part, :] = taken
        copies.append(
            pltpu.make_async_copy(master.at[part], master_out.at[part], master_sem.at[n])
        )
        copies[-1].start()
        turned = taken.T
        live_turned = at + lax.broadcasted_iota(jnp.int32, (1, size), 1) < length
        parts = []
        for b in range(4):
            block = turned[32 * b : 32 * b + 32]
            scale = jnp.maximum(jnp.max(jnp.abs(block), axis=0, keepdims=True), scale_floor)
            parts.append(block / scale)
            scales[pl.ds(b, 1), part] = jnp.where(live_turned, scale, 0.0)
        values[part, :] = jnp.concatenate(parts, axis=0).T.astype(jnp.bfloat16)
        copies.append(
            pltpu.make_async_copy(values.at[part], values_out.at[part], values_sem.at[n])
        )
        copies[-1].start()
    copies.append(pltpu.make_async_copy(scales, scales_out, sem.at[2]))
    copies[-1].start()
    for copy in copies:
        copy.wait()


def on_device(
    activations, cotangent, master_old, first_old, second_old, old_lengths, new_lengths, failed
):
    vmem = pl.BlockSpec(memory_space=pltpu.VMEM)
    smem = pl.BlockSpec(memory_space=pltpu.SMEM)
    anywhere = pl.BlockSpec(memory_space=pl.ANY)
    dma = pltpu.SemaphoreType.DMA
    wide = jax.ShapeDtypeStruct((CAP_NEW, 128), F32)
    first, second, landed, held = pl.pallas_call(
        exchange,
        out_shape=(
            pltpu.VMEM((CAP_NEW, 128), F32),
            pltpu.VMEM((CAP_NEW, 128), F32),
            pltpu.VMEM((NEW_BLOCKS * 16 + 16, 128), F32),
            pltpu.SMEM((2,), jnp.int32),
        ),
        in_specs=[anywhere] * 8,
        out_specs=(vmem, vmem, vmem, smem),
        scratch_shapes=[
            pltpu.VMEM((TOKENS, FEATURES), jnp.bfloat16),
            pltpu.VMEM((TOKENS, 128), jnp.bfloat16),
            pltpu.VMEM((128, TOKENS), jnp.bfloat16),
            pltpu.VMEM((FEATURES, 128), F32),
            pltpu.VMEM((CAP_OLD + 56, 128), F32),
            pltpu.VMEM((CAP_OLD + 56, 128), F32),
            pltpu.VMEM((CAP_OLD + 56, 128), F32),
            pltpu.VMEM((DP, SLOT_OLD, 128), F32),
            pltpu.VMEM((DP * LAND, 128), F32),
            pltpu.VMEM((DP * LAND, 128), F32),
            pltpu.VMEM((2, CHIPS, HALF, 128), F32),
            pltpu.VMEM((2, CHIPS, HALF, 128), F32),
            pltpu.VMEM((14, HALF, 128), F32),
            pltpu.VMEM((14, HALF, 128), F32),
            pltpu.VMEM((MID, 128), F32),
            pltpu.VMEM((2, 8, 128), F32),
            pltpu.VMEM((DP, 8, 128), F32),
            pltpu.VMEM((DP, 8, 128), F32),
            pltpu.VMEM((3, MID + 80, 128), F32),
            pltpu.VMEM((DP, 3, PART_NEW, 128), F32),
            pltpu.VMEM((DP, PART_NEW, 128), F32),
            pltpu.VMEM((DP, PART_NEW, 128), F32),
            pltpu.VMEM((DP, PART_NEW, 128), F32),
            pltpu.VMEM((2, NEW_BLOCKS * 16 + 16, 128), F32),
            pltpu.SMEM((DP,), jnp.int32),
            pltpu.SMEM((OLD_GROUPS,), jnp.int32),
            pltpu.SMEM((NEW_GROUPS,), jnp.int32),
            pltpu.SMEM((1,), jnp.int32),
            dma((3,)),
            dma((FEATURES // FEATURE_BLOCK,)),
            dma,
            dma((3,)),
            dma((3,)),
            dma((3, DP)),
            dma((3, DP)),
            dma((2, CHIPS)),
            dma((2, CHIPS)),
            dma((14,)),
            dma((14,)),
            dma((2 * DP,)),
            dma((2 * DP,)),
            dma((3, DP)),
            dma((3, DP)),
        ],
        compiler_params=pltpu.CompilerParams(
            collective_id=0, has_side_effects=True, vmem_limit_bytes=56 * 2**20
        ),
    )(
        activations,
        cotangent,
        master_old[0, 0],
        first_old[0, 0],
        second_old[0, 0],
        old_lengths,
        new_lengths,
        failed,
    )
    chunks = -(-CAP_NEW // 128)
    outs = pl.pallas_call(
        place,
        out_shape=(
            wide,
            wide,
            wide,
            jax.ShapeDtypeStruct((CAP_NEW, 128), jnp.bfloat16),
            jax.ShapeDtypeStruct((4, CAP_NEW), F32),
        ),
        in_specs=[vmem, vmem, vmem, smem],
        out_specs=(anywhere,) * 5,
        scratch_shapes=[
            pltpu.VMEM((CAP_NEW, 128), F32),
            pltpu.VMEM((CAP_NEW, 128), jnp.bfloat16),
            pltpu.VMEM((4, CAP_NEW), F32),
            dma((3,)),
            dma((chunks,)),
            dma((chunks,)),
        ],
        compiler_params=pltpu.CompilerParams(vmem_limit_bytes=32 * 2**20),
    )(
        *(pltpu.with_memory_space_constraint(x, pltpu.VMEM) for x in (landed, first, second)),
        pltpu.with_memory_space_constraint(held, pltpu.SMEM),
    )
    return tuple(out[None, None] for out in outs)


def solution(mesh):
    held = P("dp", "tensor", None, None)
    return jax.shard_map(
        on_device,
        mesh=mesh,
        in_specs=(P("dp", None), P("dp", "tensor"), held, held, held, P(), P(), P()),
        out_specs=(held,) * 5,
        check_vma=False,
    )
```

```python
import functools

import jax
import jax.numpy as jnp
from jax import lax
from jax.experimental import pallas as pl
from jax.experimental.pallas import tpu as pltpu
from jax.sharding import PartitionSpec as P

MESH = pl.DeviceIdType.MESH
beta_first = 0.9
beta_second = 0.95
learn_rate = 0.004
epsilon = 1e-08
scale_floor = 0.03

DP = 16
CHIPS = 8
OLD_GROUPS = 12
NEW_GROUPS = 11
FEATURES = 8192
TOKENS = 512
CAP_OLD = 1032
CAP_NEW = 1120
MID = 512
HALF = MID // 2
OLD_BLOCKS = 66
NEW_BLOCKS = 71
SLOT_OLD = 200
SLOT_NEW = 216
LAND = SLOT_OLD + 8
FEATURE_BLOCK = 512
F32 = jnp.float32

STREAMS = ((1, 0, 4), (-1, 0, 3), (-1, 1, 4), (1, 1, 3))
STREAM_BASE = (0, 4, 7, 11)
FIRST, SECOND, MASTER = 0, 1, 2
OLD_PARTS = ((0, 72), (72, 64), (136, 64))
PART_NEW = SLOT_NEW // 3
PART_1_AFTER = 3
LATE = 7
FAR_FIRST = (8, 9, 7, 10, 6, 11, 5, 12, 4, 13, 3, 14, 2, 15, 1)
SPANS = 4


def groups_near(span):
    rows = FEATURES // SPANS
    low, high = span * rows, (span + 1) * rows
    return [
        i
        for i in range(OLD_GROUPS)
        if max(i, FEATURES - CAP_OLD * (OLD_GROUPS - i)) < high and CAP_OLD * (i + 1) > low
    ]


def prefix(ref, count):
    starts, at = [], jnp.int32(0)
    for i in range(count):
        starts.append(at)
        at = at + ref[i]
    return starts


def pick(index, values):
    result = values[0]
    for i in range(1, len(values)):
        result = jnp.where(index == i, values[i], result)
    return result


def new_group(holder, lost):
    return holder - jnp.where(holder > lost, 1, 0)


def my_rows(dp, lost, new_start, new_ref):
    holder = lax.rem(dp + DP // 2, DP)
    group = jnp.clip(new_group(holder, lost), 0, NEW_GROUPS - 1)
    held = (holder != lost) & (holder < OLD_GROUPS)
    length = jnp.where(held, pick(group, [new_ref[i] for i in range(NEW_GROUPS)]), 0)
    return pick(group, new_start), length


def exchange(
    act_hbm, cot_hbm, master_hbm, first_hbm, second_hbm, old_hbm, new_hbm, lost_hbm,
    first_out, second_out, rows_master, held_out,
    act, cot_ref, cot_t, prod, state_0, state_1, state_2, send_old, land_old, held_old, sib_send, sib_land, ring_send, ring_land,
    grads, squares, squares_dp, squares_tensor, middle, send_new, land_first, land_second, land_master, rows, starts,
    old_ref, new_ref, lost_ref, table_sem,
    act_sem, cot_sem, state_sem, local_sem, old_ssem, old_rsem, sib_ssem, sib_rsem, ring_ssem, ring_rsem,
    sq_ssem, sq_rsem, new_ssem, new_rsem,
):
    dp = lax.axis_index("dp")
    tensor = lax.axis_index("tensor")
    chip = lax.div(dp, 2)
    core = lax.rem(dp, 2)

    def remote(src, dst, ssem, rsem, to_dp, to_tensor=None):
        return pltpu.make_async_remote_copy(
            src_ref=src, dst_ref=dst, send_sem=ssem, recv_sem=rsem,
            device_id=(to_dp, tensor if to_tensor is None else to_tensor),
            device_id_type=MESH,
        )

    barrier = pltpu.get_barrier_semaphore()
    for d in FAR_FIRST:
        pl.semaphore_signal(
            barrier, inc=1, device_id=(lax.rem(dp + d, DP), tensor), device_id_type=MESH
        )
    for d in FAR_FIRST:
        pl.semaphore_signal(
            barrier, inc=1, device_id=(dp, lax.rem(tensor + d, DP)), device_id_type=MESH
        )

    tables = [
        pltpu.make_async_copy(src, dst, table_sem.at[n])
        for n, (src, dst) in enumerate(
            ((old_hbm, old_ref), (new_hbm, new_ref), (lost_hbm, lost_ref))
        )
    ]
    for copy in tables:
        copy.start()
    state = (state_0, state_1, state_2)
    state_in = [
        pltpu.make_async_copy(src, state[a].at[pl.ds(16, CAP_OLD)], state_sem.at[a])
        for a, src in ((FIRST, first_hbm), (SECOND, second_hbm), (MASTER, master_hbm))
    ]
    for copy in state_in:
        copy.start()
    cot_in = pltpu.make_async_copy(cot_hbm, cot_ref, cot_sem)
    cot_in.start()
    blocks = FEATURES // FEATURE_BLOCK
    act_in = []
    for b in range(blocks):
        columns = pl.ds(b * FEATURE_BLOCK, FEATURE_BLOCK)
        act_in.append(
            pltpu.make_async_copy(act_hbm.at[:, columns], act.at[:, columns], act_sem.at[b])
        )
        act_in[-1].start()

    for copy in tables:
        copy.wait()
    lost = lost_ref[0]
    old_start = prefix(old_ref, OLD_GROUPS)
    new_start = prefix(new_ref, NEW_GROUPS)
    my_group = jnp.where(dp == OLD_GROUPS, lost, dp)
    my_old = pick(my_group, old_start)
    shift = 16 - lax.rem(my_old, 16)
    for h in range(OLD_GROUPS):
        g = jnp.clip(new_group(jnp.int32(h), lost), 0, NEW_GROUPS - 1)
        starts[(h + DP // 2) % DP] = pick(g, new_start)

    sends_old = dp <= OLD_GROUPS
    old_copies = {}
    for d in range(1, DP):
        for p, (at, size) in enumerate(OLD_PARTS):
            old_copies[d, p] = remote(
                send_old.at[d, pl.ds(at, size)],
                land_old.at[pl.ds(dp * LAND + 8 + at, size)],
                old_ssem.at[p, d], old_rsem.at[p, d], lax.rem(dp + d, DP),
            )

    def pack_old(a):
        for d in FAR_FIRST:
            send_old[d, pl.ds(a * OLD_BLOCKS, OLD_BLOCKS), :] = state[a][
                pl.ds(shift + lax.rem(dp + d, DP), OLD_BLOCKS, stride=16), :
            ]
        land_old[pl.ds(dp * LAND + 8 + a * OLD_BLOCKS, OLD_BLOCKS), :] = state[a][
            pl.ds(shift + dp, OLD_BLOCKS, stride=16), :
        ]

    def start_old(p, distances=FAR_FIRST):
        @pl.when(sends_old)
        def _():
            for d in distances:
                old_copies[d, p].start()

    def land_part(p):
        for d in range(1, DP):
            @pl.when(lax.rem(dp - d + DP, DP) <= OLD_GROUPS)
            def _():
                old_copies[d, p].wait_recv()

        at, size = OLD_PARTS[p]
        for i in range(OLD_GROUPS + 1):
            rows = pl.ds(i * LAND + 8 + at, size)
            held_old[rows, :] = land_old[rows, :]

    def pack_when(a):
        state_in[a].wait()

        @pl.when(sends_old)
        def _():
            pack_old(a)

    pack_when(FIRST)
    pack_when(SECOND)
    pl.semaphore_wait(barrier, 2 * (DP - 1))
    start_old(0)
    pack_when(MASTER)

    cot_in.wait()
    cot_t[...] = cot_ref[...].T
    sibling = dp + 1 - 2 * core
    sib_copies = {}

    def multiply(b, carry):
        columns = pl.ds(pl.multiple_of(b * FEATURE_BLOCK, FEATURE_BLOCK), FEATURE_BLOCK)
        turned = jnp.dot(cot_t[...], act[:, columns], preferred_element_type=F32)
        prod[columns, :] = turned.T
        return carry

    def chunk(off, half, which):
        c = lax.rem(chip + off, CHIPS) * 2 + which
        return prod[pl.ds(c + 16 * HALF * half, HALF, stride=16), :]

    for half in range(2):
        for b in range(blocks // 2 * half, blocks // 2 * (half + 1)):
            act_in[b].wait()
        lax.fori_loop(blocks // 2 * half, blocks // 2 * (half + 1), multiply, 0)
        for off in (4, 3, 5, 2, 6, 1, 7, 0):
            sib_send[half, off] = chunk(off, half, 1 - core)
            copy = remote(
                sib_send.at[half, off], sib_land.at[half, off],
                sib_ssem.at[half, off], sib_rsem.at[half, off], sibling,
            )
            copy.start()
            sib_copies[off, half] = copy


    arrived = set()

    def partial(off, half):
        off = off % CHIPS
        if (off, half) not in arrived:
            sib_copies[off, half].wait_recv()
            arrived.add((off, half))
        return chunk(off, half, core) + sib_land[half, off]

    ring_copies = {}
    for k in range(1, 5):
        for s, (way, half, hops) in enumerate(STREAMS):
            if k > hops:
                continue
            n = STREAM_BASE[s] + k - 1
            total = partial(way * (hops + 1 - k), half)
            if k > 1:
                ring_copies[n - 1].wait_recv()
                total = total + ring_land[n - 1]
            ring_send[n] = total
            neighbour = lax.rem(chip + way + CHIPS, CHIPS) * 2 + core
            ring_copies[n] = remote(
                ring_send.at[n], ring_land.at[n], ring_ssem.at[n], ring_rsem.at[n], neighbour
            )
            ring_copies[n].start()
        if k == PART_1_AFTER:
            start_old(1)
    ends = [STREAM_BASE[s] + STREAMS[s][2] - 1 for s in range(4)]
    square = jnp.zeros((8, 128), F32)
    for half in range(2):
        total = partial(0, half)
        for s in range(4):
            if STREAMS[s][1] == half:
                ring_copies[ends[s]].wait_recv()
                total = total + ring_land[ends[s]]
        grads[pl.ds(HALF * half, HALF), :] = total
        square = square + jnp.sum((total * total).reshape(HALF // 8, 8, 128), axis=0)

    def gather(mine, land, base, axis_dp):
        copies = []
        for d in range(1, DP):
            to_dp = lax.rem(dp + d, DP) if axis_dp else dp
            to_tensor = tensor if axis_dp else lax.rem(tensor + d, DP)
            copies.append(
                remote(
                    mine, land.at[d], sq_ssem.at[base + d], sq_rsem.at[base + d], to_dp, to_tensor
                )
            )
            copies[-1].start()
        return copies

    slots = [jnp.where(lost == i, OLD_GROUPS, i) * LAND + 8 for i in range(OLD_GROUPS)]
    old_block = [lax.div(s, 16) for s in old_start]
    old_end = [old_start[i] + old_ref[i] for i in range(OLD_GROUPS)]
    tiles = MID // 8

    def placed(base, a, near):
        row = 16 * (base + lax.broadcasted_iota(jnp.int32, (8, 128), 0)) + dp
        value = jnp.zeros((8, 128), F32)
        for i in near:
            live = (row >= old_start[i]) & (row < old_end[i])
            at = slots[i] + jnp.clip(base - old_block[i], -8, OLD_BLOCKS)
            value = jnp.where(live, held_old[pl.ds(at + a * OLD_BLOCKS, 8), :], value)
        return value

    def each_tile(body):
        for span in range(SPANS):
            near = groups_near(span)

            def step(m, carry):
                body(pl.multiple_of(m * 8, 8), near)
                return carry

            lax.fori_loop(tiles // SPANS * span, tiles // SPANS * (span + 1), step, 0)

    def settle(a):
        def body(base, near):
            middle[a, pl.ds(base, 8), :] = placed(base, a, near)

        each_tile(body)

    squares[0] = square
    first_gather = gather(squares.at[0], squares_dp, 0, True)
    start_old(2, FAR_FIRST[:LATE])
    land_part(0)
    settle(FIRST)
    for d in range(1, DP):
        first_gather[d - 1].wait_recv()
        square = square + squares_dp[d]
    squares[1] = square
    second_gather = gather(squares.at[1], squares_tensor, DP, False)
    start_old(2, FAR_FIRST[LATE:])
    land_part(1)
    settle(SECOND)
    for d in range(1, DP):
        second_gather[d - 1].wait_recv()
        square = square + squares_tensor[d]
    total = jnp.sum(jnp.sum(square, axis=1, keepdims=True), axis=0, keepdims=True)
    count_all = float(FEATURES * 128 * DP)
    clip = 1.0 / jnp.maximum(jnp.sqrt(total / count_all), 1.0)

    def holds(device):
        return (device >= DP // 2) | (device < DP // 2 + OLD_GROUPS - DP)

    new_copies = {}
    for d in range(DP):
        for a, land in enumerate((land_first, land_second, land_master)):
            if d:
                new_copies[d, a] = remote(
                    send_new.at[d, a], land.at[dp],
                    new_ssem.at[a, d], new_rsem.at[a, d], lax.rem(dp + d, DP),
                )
            else:
                new_copies[d, a] = pltpu.make_async_copy(
                    send_new.at[0, a], land.at[dp], local_sem.at[a]
                )

    def start_new(arrays):
        for d in FAR_FIRST + (0,):
            dst = lax.rem(dp + d, DP)

            @pl.when(holds(dst))
            def _():
                at = lax.div(starts[dst], 16)
                for a in arrays:
                    send_new[d, a, pl.ds(0, NEW_BLOCKS), :] = middle[
                        a, pl.ds(at, NEW_BLOCKS), :
                    ]
                    new_copies[d, a].start()

    g = clip * grads[...]
    middle[FIRST, pl.ds(0, MID), :] = (
        beta_first * middle[FIRST, pl.ds(0, MID), :] + (1.0 - beta_first) * g
    )
    start_new((FIRST,))
    middle[SECOND, pl.ds(0, MID), :] = (
        beta_second * middle[SECOND, pl.ds(0, MID), :] + (1.0 - beta_second) * g * g
    )
    start_new((SECOND,))

    correct_first = 1.0 - beta_first**10
    correct_second = 1.0 - beta_second**10
    land_part(2)

    def step_master(base, near):
        tile = pl.ds(base, 8)
        middle[MASTER, tile, :] = placed(base, MASTER, near) - learn_rate * (
            middle[FIRST, tile, :] / correct_first
        ) / (jnp.sqrt(middle[SECOND, tile, :] / correct_second) + epsilon)

    each_tile(step_master)
    start_new((MASTER,))

    @pl.when(sends_old)
    def _():
        for copy in old_copies.values():
            copy.wait_send()

    for copy in list(sib_copies.values()) + list(ring_copies.values()):
        copy.wait_send()
    for copy in first_gather + second_gather:
        copy.wait_send()

    start, length = my_rows(dp, lost, new_start, new_ref)
    held_out[0] = lax.rem(start, 16)
    held_out[1] = length

    def land_new(a, land, out):
        @pl.when(holds(dp))
        def _():
            for d in (0, 1, 15, 2, 14, 3, 13, 4, 12, 5, 11, 6, 10, 7, 9, 8):
                if d:
                    new_copies[d, a].wait_recv()
                else:
                    new_copies[0, a].wait()
                c = lax.rem(dp - d + DP, DP)
                out[pl.ds(c, NEW_BLOCKS, stride=16), :] = land[c, pl.ds(0, NEW_BLOCKS), :]

    for a, land, out in ((FIRST, land_first, first_out), (SECOND, land_second, second_out)):
        land_new(a, land, rows.at[a])
        for at in range(0, CAP_NEW, 160):
            live = at + lax.broadcasted_iota(jnp.int32, (160, 128), 0) < length
            taken = rows[a, pl.ds(lax.rem(start, 16) + at, 160), :]
            out[pl.ds(at, 160), :] = jnp.where(live, taken, 0.0)
    for d in range(1, DP):
        @pl.when(holds(lax.rem(dp + d, DP)))
        def _():
            for a in range(3):
                new_copies[d, a].wait_send()

    land_new(MASTER, land_master, rows_master)


def place(
    rows, first, second, held_ref,
    master_out, first_out, second_out, values_out, scales_out,
    master, values, scales, sem, master_sem, values_sem,
):
    copies = [
        pltpu.make_async_copy(first, first_out, sem.at[0]),
        pltpu.make_async_copy(second, second_out, sem.at[1]),
    ]
    for copy in copies:
        copy.start()
    offset = held_ref[0]
    length = held_ref[1]
    step = 128
    for n, at in enumerate(range(0, CAP_NEW, step)):
        size = min(step, CAP_NEW - at)
        part = pl.ds(at, size)
        live = at + lax.broadcasted_iota(jnp.int32, (size, 128), 0) < length
        taken = jnp.where(live, rows[pl.ds(offset + at, size), :], 0.0)
        master[part, :] = taken
        copies.append(
            pltpu.make_async_copy(master.at[part], master_out.at[part], master_sem.at[n])
        )
        copies[-1].start()
        turned = taken.T
        live_turned = at + lax.broadcasted_iota(jnp.int32, (1, size), 1) < length
        parts = []
        for b in range(4):
            block = turned[32 * b : 32 * b + 32]
            scale = jnp.maximum(jnp.max(jnp.abs(block), axis=0, keepdims=True), scale_floor)
            parts.append(block / scale)
            scales[pl.ds(b, 1), part] = jnp.where(live_turned, scale, 0.0)
        values[part, :] = jnp.concatenate(parts, axis=0).T.astype(jnp.bfloat16)
        copies.append(
            pltpu.make_async_copy(values.at[part], values_out.at[part], values_sem.at[n])
        )
        copies[-1].start()
    copies.append(pltpu.make_async_copy(scales, scales_out, sem.at[2]))
    copies[-1].start()
    for copy in copies:
        copy.wait()


def on_device(
    activations, cotangent, master_old, first_old, second_old, old_lengths, new_lengths, failed
):
    vmem = pl.BlockSpec(memory_space=pltpu.VMEM)
    smem = pl.BlockSpec(memory_space=pltpu.SMEM)
    anywhere = pl.BlockSpec(memory_space=pl.ANY)
    dma = pltpu.SemaphoreType.DMA
    wide = jax.ShapeDtypeStruct((CAP_NEW, 128), F32)
    first, second, landed, held = pl.pallas_call(
        exchange,
        out_shape=(
            pltpu.VMEM((CAP_NEW, 128), F32),
            pltpu.VMEM((CAP_NEW, 128), F32),
            pltpu.VMEM((NEW_BLOCKS * 16 + 16, 128), F32),
            pltpu.SMEM((2,), jnp.int32),
        ),
        in_specs=[anywhere] * 8,
        out_specs=(vmem, vmem, vmem, smem),
        scratch_shapes=[
            pltpu.VMEM((TOKENS, FEATURES), jnp.bfloat16),
            pltpu.VMEM((TOKENS, 128), jnp.bfloat16),
            pltpu.VMEM((128, TOKENS), jnp.bfloat16),
            pltpu.VMEM((FEATURES + 16, 128), F32),
            pltpu.VMEM((CAP_OLD + 56, 128), F32),
            pltpu.VMEM((CAP_OLD + 56, 128), F32),
            pltpu.VMEM((CAP_OLD + 56, 128), F32),
            pltpu.VMEM((DP, SLOT_OLD, 128), F32),
            pltpu.VMEM((DP * LAND, 128), F32),
            pltpu.VMEM((DP * LAND, 128), F32),
            pltpu.VMEM((2, CHIPS, HALF, 128), F32),
            pltpu.VMEM((2, CHIPS, HALF, 128), F32),
            pltpu.VMEM((14, HALF, 128), F32),
            pltpu.VMEM((14, HALF, 128), F32),
            pltpu.VMEM((MID, 128), F32),
            pltpu.VMEM((2, 8, 128), F32),
            pltpu.VMEM((DP, 8, 128), F32),
            pltpu.VMEM((DP, 8, 128), F32),
            pltpu.VMEM((3, MID + 80, 128), F32),
            pltpu.VMEM((DP, 3, PART_NEW, 128), F32),
            pltpu.VMEM((DP, PART_NEW, 128), F32),
            pltpu.VMEM((DP, PART_NEW, 128), F32),
            pltpu.VMEM((DP, PART_NEW, 128), F32),
            pltpu.VMEM((2, NEW_BLOCKS * 16 + 16, 128), F32),
            pltpu.SMEM((DP,), jnp.int32),
            pltpu.SMEM((OLD_GROUPS,), jnp.int32),
            pltpu.SMEM((NEW_GROUPS,), jnp.int32),
            pltpu.SMEM((1,), jnp.int32),
            dma((3,)),
            dma((FEATURES // FEATURE_BLOCK,)),
            dma,
            dma((3,)),
            dma((3,)),
            dma((3, DP)),
            dma((3, DP)),
            dma((2, CHIPS)),
            dma((2, CHIPS)),
            dma((14,)),
            dma((14,)),
            dma((2 * DP,)),
            dma((2 * DP,)),
            dma((3, DP)),
            dma((3, DP)),
        ],
        compiler_params=pltpu.CompilerParams(
            collective_id=0, has_side_effects=True, vmem_limit_bytes=56 * 2**20
        ),
    )(
        activations,
        cotangent,
        master_old[0, 0],
        first_old[0, 0],
        second_old[0, 0],
        old_lengths,
        new_lengths,
        failed,
    )
    chunks = -(-CAP_NEW // 128)
    outs = pl.pallas_call(
        place,
        out_shape=(
            wide,
            wide,
            wide,
            jax.ShapeDtypeStruct((CAP_NEW, 128), jnp.bfloat16),
            jax.ShapeDtypeStruct((4, CAP_NEW), F32),
        ),
        in_specs=[vmem, vmem, vmem, smem],
        out_specs=(anywhere,) * 5,
        scratch_shapes=[
            pltpu.VMEM((CAP_NEW, 128), F32),
            pltpu.VMEM((CAP_NEW, 128), jnp.bfloat16),
            pltpu.VMEM((4, CAP_NEW), F32),
            dma((3,)),
            dma((chunks,)),
            dma((chunks,)),
        ],
        compiler_params=pltpu.CompilerParams(vmem_limit_bytes=32 * 2**20),
    )(
        *(pltpu.with_memory_space_constraint(x, pltpu.VMEM) for x in (landed, first, second)),
        pltpu.with_memory_space_constraint(held, pltpu.SMEM),
    )
    return tuple(out[None, None] for out in outs)


def solution(mesh):
    held = P("dp", "tensor", None, None)
    return jax.shard_map(
        on_device,
        mesh=mesh,
        in_specs=(P("dp", None), P("dp", "tensor"), held, held, held, P(), P(), P()),
        out_specs=(held,) * 5,
        check_vma=False,
    )
```

```python
import functools

import jax
import jax.numpy as jnp
from jax import lax
from jax.experimental import pallas as pl
from jax.experimental.pallas import tpu as pltpu
from jax.sharding import PartitionSpec as P

MESH = pl.DeviceIdType.MESH
beta_first = 0.9
beta_second = 0.95
learn_rate = 0.004
epsilon = 1e-08
scale_floor = 0.03

DP = 16
CHIPS = 8
OLD_GROUPS = 12
NEW_GROUPS = 11
FEATURES = 8192
TOKENS = 512
CAP_OLD = 1032
CAP_NEW = 1120
MID = 512
HALF = MID // 2
OLD_BLOCKS = 66
NEW_BLOCKS = 71
SLOT_OLD = 200
SLOT_NEW = 216
LAND = SLOT_OLD + 8
FEATURE_BLOCK = 512
F32 = jnp.float32

STREAMS = ((1, 0, 4), (-1, 0, 3), (-1, 1, 4), (1, 1, 3))
STREAM_BASE = (0, 4, 7, 11)
FIRST, SECOND, MASTER = 0, 1, 2
OLD_PARTS = ((0, 72), (72, 64), (136, 64))
PART_NEW = SLOT_NEW // 3
PART_1_AFTER = 3
LATE = 7
FAR_FIRST = (8, 9, 7, 10, 6, 11, 5, 12, 4, 13, 3, 14, 2, 15, 1)
SPANS = 4


def groups_near(span):
    rows = FEATURES // SPANS
    low, high = span * rows, (span + 1) * rows
    return [
        i
        for i in range(OLD_GROUPS)
        if max(i, FEATURES - CAP_OLD * (OLD_GROUPS - i)) < high and CAP_OLD * (i + 1) > low
    ]


def prefix(ref, count):
    starts, at = [], jnp.int32(0)
    for i in range(count):
        starts.append(at)
        at = at + ref[i]
    return starts


def pick(index, values):
    result = values[0]
    for i in range(1, len(values)):
        result = jnp.where(index == i, values[i], result)
    return result


def new_group(holder, lost):
    return holder - jnp.where(holder > lost, 1, 0)


def my_rows(dp, lost, new_start, new_ref):
    holder = lax.rem(dp + DP // 2, DP)
    group = jnp.clip(new_group(holder, lost), 0, NEW_GROUPS - 1)
    held = (holder != lost) & (holder < OLD_GROUPS)
    length = jnp.where(held, pick(group, [new_ref[i] for i in range(NEW_GROUPS)]), 0)
    return pick(group, new_start), length


def exchange(
    act_hbm, cot_hbm, master_hbm, first_hbm, second_hbm, old_hbm, new_hbm, lost_hbm,
    first_out, second_out, rows_master, held_out,
    act, cot_ref, cot_t, prod, state_0, state_1, state_2, send_old, land_old, held_old, sib_send, sib_land, ring_send, ring_land,
    grads, squares, squares_dp, squares_tensor, middle, send_new, land_first, land_second, land_master, rows, starts,
    old_ref, new_ref, lost_ref, table_sem,
    act_sem, cot_sem, state_sem, local_sem, old_ssem, old_rsem, sib_ssem, sib_rsem, ring_ssem, ring_rsem,
    sq_ssem, sq_rsem, new_ssem, new_rsem,
):
    dp = lax.axis_index("dp")
    tensor = lax.axis_index("tensor")
    chip = lax.div(dp, 2)
    core = lax.rem(dp, 2)

    def remote(src, dst, ssem, rsem, to_dp, to_tensor=None):
        return pltpu.make_async_remote_copy(
            src_ref=src, dst_ref=dst, send_sem=ssem, recv_sem=rsem,
            device_id=(to_dp, tensor if to_tensor is None else to_tensor),
            device_id_type=MESH,
        )

    barrier = pltpu.get_barrier_semaphore()
    for d in FAR_FIRST:
        pl.semaphore_signal(
            barrier, inc=1, device_id=(lax.rem(dp + d, DP), tensor), device_id_type=MESH
        )
    for d in FAR_FIRST:
        pl.semaphore_signal(
            barrier, inc=1, device_id=(dp, lax.rem(tensor + d, DP)), device_id_type=MESH
        )

    tables = [
        pltpu.make_async_copy(src, dst, table_sem.at[n])
        for n, (src, dst) in enumerate(
            ((old_hbm, old_ref), (new_hbm, new_ref), (lost_hbm, lost_ref))
        )
    ]
    for copy in tables:
        copy.start()
    state = (state_0, state_1, state_2)
    state_in = [
        pltpu.make_async_copy(src, state[a].at[pl.ds(16, CAP_OLD)], state_sem.at[a])
        for a, src in ((FIRST, first_hbm), (SECOND, second_hbm), (MASTER, master_hbm))
    ]
    for copy in state_in:
        copy.start()
    cot_in = pltpu.make_async_copy(cot_hbm, cot_ref, cot_sem)
    cot_in.start()
    blocks = FEATURES // FEATURE_BLOCK
    act_in = []
    for b in range(blocks):
        columns = pl.ds(b * FEATURE_BLOCK, FEATURE_BLOCK)
        act_in.append(
            pltpu.make_async_copy(act_hbm.at[:, columns], act.at[:, columns], act_sem.at[b])
        )
        act_in[-1].start()

    for copy in tables:
        copy.wait()
    lost = lost_ref[0]
    old_start = prefix(old_ref, OLD_GROUPS)
    new_start = prefix(new_ref, NEW_GROUPS)
    my_group = jnp.where(dp == OLD_GROUPS, lost, dp)
    my_old = pick(my_group, old_start)
    shift = 16 - lax.rem(my_old, 16)
    for h in range(OLD_GROUPS):
        g = jnp.clip(new_group(jnp.int32(h), lost), 0, NEW_GROUPS - 1)
        starts[(h + DP // 2) % DP] = pick(g, new_start)

    sends_old = dp <= OLD_GROUPS
    old_copies = {}
    for d in range(1, DP):
        for p, (at, size) in enumerate(OLD_PARTS):
            old_copies[d, p] = remote(
                send_old.at[d, pl.ds(at, size)],
                land_old.at[pl.ds(dp * LAND + 8 + at, size)],
                old_ssem.at[p, d], old_rsem.at[p, d], lax.rem(dp + d, DP),
            )

    def pack_old(a):
        for d in FAR_FIRST:
            send_old[d, pl.ds(a * OLD_BLOCKS, OLD_BLOCKS), :] = state[a][
                pl.ds(shift + lax.rem(dp + d, DP), OLD_BLOCKS, stride=16), :
            ]
        land_old[pl.ds(dp * LAND + 8 + a * OLD_BLOCKS, OLD_BLOCKS), :] = state[a][
            pl.ds(shift + dp, OLD_BLOCKS, stride=16), :
        ]

    def start_old(p, distances=FAR_FIRST):
        @pl.when(sends_old)
        def _():
            for d in distances:
                old_copies[d, p].start()

    def land_part(p):
        for d in range(1, DP):
            @pl.when(lax.rem(dp - d + DP, DP) <= OLD_GROUPS)
            def _():
                old_copies[d, p].wait_recv()

        at, size = OLD_PARTS[p]
        for i in range(OLD_GROUPS + 1):
            rows = pl.ds(i * LAND + 8 + at, size)
            held_old[rows, :] = land_old[rows, :]

    def pack_when(a):
        state_in[a].wait()

        @pl.when(sends_old)
        def _():
            pack_old(a)

    pack_when(FIRST)
    pack_when(SECOND)
    pl.semaphore_wait(barrier, 2 * (DP - 1))
    start_old(0)
    pack_when(MASTER)

    cot_in.wait()
    cot_t[...] = cot_ref[...].T
    sibling = dp + 1 - 2 * core
    sib_copies = {}

    def multiply(b, carry):
        columns = pl.ds(pl.multiple_of(b * FEATURE_BLOCK, FEATURE_BLOCK), FEATURE_BLOCK)
        turned = jnp.dot(cot_t[...], act[:, columns], preferred_element_type=F32)
        prod[columns, :] = turned.T
        return carry

    def chunk(off, half, which):
        c = lax.rem(chip + off, CHIPS) * 2 + which
        return prod[pl.ds(c + 16 * HALF * half, HALF, stride=16), :]

    for half in range(2):
        for b in range(blocks // 2 * half, blocks // 2 * (half + 1)):
            act_in[b].wait()
        lax.fori_loop(blocks // 2 * half, blocks // 2 * (half + 1), multiply, 0)
        for off in (4, 3, 5, 2, 6, 1, 7, 0):
            sib_send[half, off] = chunk(off, half, 1 - core)
            copy = remote(
                sib_send.at[half, off], sib_land.at[half, off],
                sib_ssem.at[half, off], sib_rsem.at[half, off], sibling,
            )
            copy.start()
            sib_copies[off, half] = copy


    arrived = set()

    def partial(off, half):
        off = off % CHIPS
        if (off, half) not in arrived:
            sib_copies[off, half].wait_recv()
            arrived.add((off, half))
        return chunk(off, half, core) + sib_land[half, off]

    ring_copies = {}
    for k in range(1, 5):
        for s, (way, half, hops) in enumerate(STREAMS):
            if k > hops:
                continue
            n = STREAM_BASE[s] + k - 1
            total = partial(way * (hops + 1 - k), half)
            if k > 1:
                ring_copies[n - 1].wait_recv()
                total = total + ring_land[n - 1]
            ring_send[n] = total
            neighbour = lax.rem(chip + way + CHIPS, CHIPS) * 2 + core
            ring_copies[n] = remote(
                ring_send.at[n], ring_land.at[n], ring_ssem.at[n], ring_rsem.at[n], neighbour
            )
            ring_copies[n].start()
        if k == PART_1_AFTER:
            start_old(1)
    ends = [STREAM_BASE[s] + STREAMS[s][2] - 1 for s in range(4)]
    square = jnp.zeros((8, 128), F32)
    for half in range(2):
        total = partial(0, half)
        for s in range(4):
            if STREAMS[s][1] == half:
                ring_copies[ends[s]].wait_recv()
                total = total + ring_land[ends[s]]
        grads[pl.ds(HALF * half, HALF), :] = total
        square = square + jnp.sum((total * total).reshape(HALF // 8, 8, 128), axis=0)

    def gather(mine, land, base, axis_dp):
        copies = []
        for d in range(1, DP):
            to_dp = lax.rem(dp + d, DP) if axis_dp else dp
            to_tensor = tensor if axis_dp else lax.rem(tensor + d, DP)
            copies.append(
                remote(
                    mine, land.at[d], sq_ssem.at[base + d], sq_rsem.at[base + d], to_dp, to_tensor
                )
            )
            copies[-1].start()
        return copies

    slots = [jnp.where(lost == i, OLD_GROUPS, i) * LAND + 8 for i in range(OLD_GROUPS)]
    old_block = [lax.div(s, 16) for s in old_start]
    old_end = [old_start[i] + old_ref[i] for i in range(OLD_GROUPS)]
    tiles = MID // 8

    def placed(base, a, near):
        row = 16 * (base + lax.broadcasted_iota(jnp.int32, (8, 128), 0)) + dp
        value = jnp.zeros((8, 128), F32)
        for i in near:
            live = (row >= old_start[i]) & (row < old_end[i])
            at = slots[i] + jnp.clip(base - old_block[i], -8, OLD_BLOCKS)
            value = jnp.where(live, held_old[pl.ds(at + a * OLD_BLOCKS, 8), :], value)
        return value

    def each_tile(body):
        for span in range(SPANS):
            near = groups_near(span)

            def step(m, carry):
                body(pl.multiple_of(m * 8, 8), near)
                return carry

            lax.fori_loop(tiles // SPANS * span, tiles // SPANS * (span + 1), step, 0)

    def settle(a):
        def body(base, near):
            middle[a, pl.ds(base, 8), :] = placed(base, a, near)

        each_tile(body)

    squares[0] = square
    first_gather = gather(squares.at[0], squares_dp, 0, True)
    start_old(2, FAR_FIRST[:LATE])
    land_part(0)
    settle(FIRST)
    for d in range(1, DP):
        first_gather[d - 1].wait_recv()
        square = square + squares_dp[d]
    squares[1] = square
    second_gather = gather(squares.at[1], squares_tensor, DP, False)
    start_old(2, FAR_FIRST[LATE:])
    for d in range(1, DP):
        second_gather[d - 1].wait_recv()
        square = square + squares_tensor[d]
    total = jnp.sum(jnp.sum(square, axis=1, keepdims=True), axis=0, keepdims=True)
    count_all = float(FEATURES * 128 * DP)
    clip = 1.0 / jnp.maximum(jnp.sqrt(total / count_all), 1.0)

    def holds(device):
        return (device >= DP // 2) | (device < DP // 2 + OLD_GROUPS - DP)

    new_copies = {}
    for d in range(DP):
        for a, land in enumerate((land_first, land_second, land_master)):
            if d:
                new_copies[d, a] = remote(
                    send_new.at[d, a], land.at[dp],
                    new_ssem.at[a, d], new_rsem.at[a, d], lax.rem(dp + d, DP),
                )
            else:
                new_copies[d, a] = pltpu.make_async_copy(
                    send_new.at[0, a], land.at[dp], local_sem.at[a]
                )

    def start_new(arrays):
        for d in FAR_FIRST + (0,):
            dst = lax.rem(dp + d, DP)

            @pl.when(holds(dst))
            def _():
                at = lax.div(starts[dst], 16)
                for a in arrays:
                    send_new[d, a, pl.ds(0, NEW_BLOCKS), :] = middle[
                        a, pl.ds(at, NEW_BLOCKS), :
                    ]
                    new_copies[d, a].start()

    g = clip * grads[...]
    middle[FIRST, pl.ds(0, MID), :] = (
        beta_first * middle[FIRST, pl.ds(0, MID), :] + (1.0 - beta_first) * g
    )
    start_new((FIRST,))
    land_part(1)
    settle(SECOND)
    middle[SECOND, pl.ds(0, MID), :] = (
        beta_second * middle[SECOND, pl.ds(0, MID), :] + (1.0 - beta_second) * g * g
    )
    start_new((SECOND,))

    correct_first = 1.0 - beta_first**10
    correct_second = 1.0 - beta_second**10
    land_part(2)

    def step_master(base, near):
        tile = pl.ds(base, 8)
        middle[MASTER, tile, :] = placed(base, MASTER, near) - learn_rate * (
            middle[FIRST, tile, :] / correct_first
        ) / (jnp.sqrt(middle[SECOND, tile, :] / correct_second) + epsilon)

    each_tile(step_master)
    start_new((MASTER,))

    @pl.when(sends_old)
    def _():
        for copy in old_copies.values():
            copy.wait_send()

    for copy in list(sib_copies.values()) + list(ring_copies.values()):
        copy.wait_send()
    for copy in first_gather + second_gather:
        copy.wait_send()

    start, length = my_rows(dp, lost, new_start, new_ref)
    held_out[0] = lax.rem(start, 16)
    held_out[1] = length

    def land_new(a, land, out):
        @pl.when(holds(dp))
        def _():
            for d in (0, 1, 15, 2, 14, 3, 13, 4, 12, 5, 11, 6, 10, 7, 9, 8):
                if d:
                    new_copies[d, a].wait_recv()
                else:
                    new_copies[0, a].wait()
                c = lax.rem(dp - d + DP, DP)
                out[pl.ds(c, NEW_BLOCKS, stride=16), :] = land[c, pl.ds(0, NEW_BLOCKS), :]

    for a, land, out in ((FIRST, land_first, first_out), (SECOND, land_second, second_out)):
        land_new(a, land, rows.at[a])
        for at in range(0, CAP_NEW, 160):
            live = at + lax.broadcasted_iota(jnp.int32, (160, 128), 0) < length
            taken = rows[a, pl.ds(lax.rem(start, 16) + at, 160), :]
            out[pl.ds(at, 160), :] = jnp.where(live, taken, 0.0)
    for d in range(1, DP):
        @pl.when(holds(lax.rem(dp + d, DP)))
        def _():
            for a in range(3):
                new_copies[d, a].wait_send()

    land_new(MASTER, land_master, rows_master)


def place(
    rows, first, second, held_ref,
    master_out, first_out, second_out, values_out, scales_out,
    master, values, scales, sem, master_sem, values_sem,
):
    copies = [
        pltpu.make_async_copy(first, first_out, sem.at[0]),
        pltpu.make_async_copy(second, second_out, sem.at[1]),
    ]
    for copy in copies:
        copy.start()
    offset = held_ref[0]
    length = held_ref[1]
    step = 128
    for n, at in enumerate(range(0, CAP_NEW, step)):
        size = min(step, CAP_NEW - at)
        part = pl.ds(at, size)
        live = at + lax.broadcasted_iota(jnp.int32, (size, 128), 0) < length
        taken = jnp.where(live, rows[pl.ds(offset + at, size), :], 0.0)
        master[part, :] = taken
        copies.append(
            pltpu.make_async_copy(master.at[part], master_out.at[part], master_sem.at[n])
        )
        copies[-1].start()
        turned = taken.T
        live_turned = at + lax.broadcasted_iota(jnp.int32, (1, size), 1) < length
        parts = []
        for b in range(4):
            block = turned[32 * b : 32 * b + 32]
            scale = jnp.maximum(jnp.max(jnp.abs(block), axis=0, keepdims=True), scale_floor)
            parts.append(block / scale)
            scales[pl.ds(b, 1), part] = jnp.where(live_turned, scale, 0.0)
        values[part, :] = jnp.concatenate(parts, axis=0).T.astype(jnp.bfloat16)
        copies.append(
            pltpu.make_async_copy(values.at[part], values_out.at[part], values_sem.at[n])
        )
        copies[-1].start()
    copies.append(pltpu.make_async_copy(scales, scales_out, sem.at[2]))
    copies[-1].start()
    for copy in copies:
        copy.wait()


def on_device(
    activations, cotangent, master_old, first_old, second_old, old_lengths, new_lengths, failed
):
    vmem = pl.BlockSpec(memory_space=pltpu.VMEM)
    smem = pl.BlockSpec(memory_space=pltpu.SMEM)
    anywhere = pl.BlockSpec(memory_space=pl.ANY)
    dma = pltpu.SemaphoreType.DMA
    wide = jax.ShapeDtypeStruct((CAP_NEW, 128), F32)
    first, second, landed, held = pl.pallas_call(
        exchange,
        out_shape=(
            pltpu.VMEM((CAP_NEW, 128), F32),
            pltpu.VMEM((CAP_NEW, 128), F32),
            pltpu.VMEM((NEW_BLOCKS * 16 + 16, 128), F32),
            pltpu.SMEM((2,), jnp.int32),
        ),
        in_specs=[anywhere] * 8,
        out_specs=(vmem, vmem, vmem, smem),
        scratch_shapes=[
            pltpu.VMEM((TOKENS, FEATURES), jnp.bfloat16),
            pltpu.VMEM((TOKENS, 128), jnp.bfloat16),
            pltpu.VMEM((128, TOKENS), jnp.bfloat16),
            pltpu.VMEM((FEATURES + 16, 128), F32),
            pltpu.VMEM((CAP_OLD + 56, 128), F32),
            pltpu.VMEM((CAP_OLD + 56, 128), F32),
            pltpu.VMEM((CAP_OLD + 56, 128), F32),
            pltpu.VMEM((DP, SLOT_OLD, 128), F32),
            pltpu.VMEM((DP * LAND, 128), F32),
            pltpu.VMEM((DP * LAND, 128), F32),
            pltpu.VMEM((2, CHIPS, HALF, 128), F32),
            pltpu.VMEM((2, CHIPS, HALF, 128), F32),
            pltpu.VMEM((14, HALF, 128), F32),
            pltpu.VMEM((14, HALF, 128), F32),
            pltpu.VMEM((MID, 128), F32),
            pltpu.VMEM((2, 8, 128), F32),
            pltpu.VMEM((DP, 8, 128), F32),
            pltpu.VMEM((DP, 8, 128), F32),
            pltpu.VMEM((3, MID + 80, 128), F32),
            pltpu.VMEM((DP, 3, PART_NEW, 128), F32),
            pltpu.VMEM((DP, PART_NEW, 128), F32),
            pltpu.VMEM((DP, PART_NEW, 128), F32),
            pltpu.VMEM((DP, PART_NEW, 128), F32),
            pltpu.VMEM((2, NEW_BLOCKS * 16 + 16, 128), F32),
            pltpu.SMEM((DP,), jnp.int32),
            pltpu.SMEM((OLD_GROUPS,), jnp.int32),
            pltpu.SMEM((NEW_GROUPS,), jnp.int32),
            pltpu.SMEM((1,), jnp.int32),
            dma((3,)),
            dma((FEATURES // FEATURE_BLOCK,)),
            dma,
            dma((3,)),
            dma((3,)),
            dma((3, DP)),
            dma((3, DP)),
            dma((2, CHIPS)),
            dma((2, CHIPS)),
            dma((14,)),
            dma((14,)),
            dma((2 * DP,)),
            dma((2 * DP,)),
            dma((3, DP)),
            dma((3, DP)),
        ],
        compiler_params=pltpu.CompilerParams(
            collective_id=0, has_side_effects=True, vmem_limit_bytes=56 * 2**20
        ),
    )(
        activations,
        cotangent,
        master_old[0, 0],
        first_old[0, 0],
        second_old[0, 0],
        old_lengths,
        new_lengths,
        failed,
    )
    chunks = -(-CAP_NEW // 128)
    outs = pl.pallas_call(
        place,
        out_shape=(
            wide,
            wide,
            wide,
            jax.ShapeDtypeStruct((CAP_NEW, 128), jnp.bfloat16),
            jax.ShapeDtypeStruct((4, CAP_NEW), F32),
        ),
        in_specs=[vmem, vmem, vmem, smem],
        out_specs=(anywhere,) * 5,
        scratch_shapes=[
            pltpu.VMEM((CAP_NEW, 128), F32),
            pltpu.VMEM((CAP_NEW, 128), jnp.bfloat16),
            pltpu.VMEM((4, CAP_NEW), F32),
            dma((3,)),
            dma((chunks,)),
            dma((chunks,)),
        ],
        compiler_params=pltpu.CompilerParams(vmem_limit_bytes=32 * 2**20),
    )(
        *(pltpu.with_memory_space_constraint(x, pltpu.VMEM) for x in (landed, first, second)),
        pltpu.with_memory_space_constraint(held, pltpu.SMEM),
    )
    return tuple(out[None, None] for out in outs)


def solution(mesh):
    held = P("dp", "tensor", None, None)
    return jax.shard_map(
        on_device,
        mesh=mesh,
        in_specs=(P("dp", None), P("dp", "tensor"), held, held, held, P(), P(), P()),
        out_specs=(held,) * 5,
        check_vma=False,
    )
```
